32 devices in a mesh: chan: 8 (over z, y), rows: 4 (over x, core).
Axes of the slice: x: 2, y: 2, z: 4, core: 2. Of those that a mesh axis runs over, the one named last changes fastest.
Arguments:
- activations: bfloat16 [1024, 8, 256], P('chan', 'rows'), may hold values from -6 to 6
- weights: bfloat16 [3, 3, 1024, 1024], P(None, None, 'chan'), may hold values from -0.0625 to 0.0625
- cotangent: bfloat16 [1024, 8, 256], P('chan', 'rows'), may hold values from -6 to 6
Outputs:
- output_map: bfloat16 [1024, 8, 256], P('chan', 'rows')
- input_grad: bfloat16 [1024, 8, 256], P('chan', 'rows')
- filter_grad: float32 [3, 3, 1024, 1024], P(None, None, ('chan', 'rows'))
The draws below stay inside these ranges and needn't reach their ends.
All inputs are finite; a program needn't handle non-finite values.
Results may differ from the reference program's by a relative error of at most 0.001.
Values may be sent and summed in bfloat16 or wider, within the bound.
No kernel may reach another device: no remote copies, remote signals or barrier semaphores. Data moves between devices by JAX's collectives and lax.ppermute only.
A program may use at most 64 MiB of HBM per device.

```python
import math
import jax
import jax.numpy as jnp
from jax import lax

C = 1024
W = 256
HEIGHT = 8


def spiked(array, stream_key, source, target, blocks, factor):
    owner, partner = [(jnp.arange(array.shape[dim]) // (array.shape[dim] // blocks)).reshape([-1 if axis == dim else 1 for axis in range(array.ndim)]) for dim in (source, target)]
    chosen = jax.random.permutation(stream_key, blocks)[partner]
    strong = (owner == chosen) | (owner == (partner + blocks // 2) % blocks)
    return jnp.where(strong, factor * array, array)


def levels(key, shape, cuts, least, largest):
    gain = 1.0
    for dim, parts in cuts:
        steps = jax.random.uniform(jax.random.fold_in(jax.random.fold_in(key, 6), dim), (parts,), jnp.float32, least / len(cuts), largest / len(cuts))
        gain = gain * jnp.repeat(jnp.exp(steps), shape[dim] // parts).reshape((-1,) + (1,) * (len(shape) - 1 - dim))
    return gain


def centred(stream_key, shape, spread, limit, pieces=(), dtype=jnp.bfloat16):
    entries = jax.random.normal(stream_key, shape, jnp.float32) * spread
    if len(pieces) > 0:
        entries = levels(stream_key, shape, pieces, -0.22, 0.18) * entries
    return jnp.clip(entries, min=-limit, max=limit).astype(dtype)


def gaussian_with(rng, shape, deviation, most, pieces, heavy, kind=jnp.bfloat16):
    result = deviation * jax.random.normal(rng, shape, jnp.float32)
    if pieces:
        result = result * levels(rng, shape, pieces, -0.22, 0.18)
    return jnp.clip(spiked(result, jax.random.fold_in(rng, 3), *heavy), -most, most).astype(kind)


def setup_inputs(seed: int = 0) -> dict:
    key_list = jax.random.split(jax.random.key(seed), 4)
    activations = centred(key_list[0], (C, HEIGHT, W), 1.0, 6.0, ((0, 8), (1, 4)))
    weights = centred(key_list[1], (3, 3, C, C), (9 * C) ** -0.5, 0.0625, ((2, 8),))
    cotangent = gaussian_with(key_list[2], (C, HEIGHT, W), 1.0, 6.0, ((0, 8), (1, 4)), (1, 0, 8, 2.0))
    return dict(activations=activations, weights=weights, cotangent=cotangent)


def shift_columns(values, offset):
    if offset == 0:
        return values
    extent = values.shape[-1]
    widths = [(0, 0)] * (values.ndim - 1)
    if offset > 0:
        return jnp.pad(values[..., offset:], widths + [(0, offset)])
    return jnp.pad(values[..., :extent + offset], widths + [(-offset, 0)])

def matmul(left, right):
    return jnp.dot(left, right, preferred_element_type=jnp.float32, precision=lax.Precision.HIGHEST)

def reference(activations, weights, cotangent):
    xfull = activations.astype(jnp.float32)
    gfull = cotangent.astype(jnp.float32)
    wfull = weights.astype(jnp.float32)
    channels, height, width = xfull.shape
    xpadded = jnp.pad(xfull, ((0, 0), (1, 1), (0, 0)))
    gpadded = jnp.pad(gfull, ((0, 0), (1, 1), (0, 0)))
    output = jnp.zeros((channels, height, width), jnp.float32)
    grad_in = jnp.zeros((channels, height, width), jnp.float32)
    filters = []
    for tap_col in range(3):
        forward_part = jnp.zeros((channels, height * width), jnp.float32)
        back_part = jnp.zeros((channels, height * width), jnp.float32)
        for tap_row in range(3):
            xslab = xpadded[:, tap_row:tap_row + height].reshape(channels, height * width)
            gslab = gpadded[:, 2 - tap_row:2 - tap_row + height].reshape(channels, height * width)
            forward_part = forward_part + matmul(wfull[tap_row, tap_col], xslab)
            back_part = back_part + matmul(wfull[tap_row, tap_col].T, gslab)
        output = output + shift_columns(forward_part.reshape(channels, height, width), tap_col - 1)
        grad_in = grad_in + shift_columns(back_part.reshape(channels, height, width), 1 - tap_col)
    for tap_row in range(3):
        xslab = xpadded[:, tap_row:tap_row + height].reshape(channels, height * width)
        line = []
        for tap_col in range(3):
            gshift = shift_columns(gfull, 1 - tap_col).reshape(channels, height * width)
            line.append(matmul(gshift, xslab.T))
        filters.append(jnp.stack(line))
    scale = 1.0 / math.sqrt(height * width)
    filter_grad = jnp.stack(filters) * scale
    return (output.astype(jnp.bfloat16), grad_in.astype(jnp.bfloat16), filter_grad)
```

```python
import math

import jax
import jax.numpy as jnp
from jax import lax
from jax.sharding import PartitionSpec as P

BF16, F32 = jnp.bfloat16, jnp.float32
SPAN = 124.0
LEAST = 2.0**-100


def exchange(x, axis, distance):
    size = lax.axis_size(axis)
    return lax.ppermute(x, axis, [(i, i ^ distance) for i in range(size)])


def shift_columns(values, offset):
    if offset == 0:
        return values
    extent = values.shape[-1]
    widths = [(0, 0)] * (values.ndim - 1)
    if offset > 0:
        return jnp.pad(values[..., offset:], widths + [(0, offset)])
    return jnp.pad(values[..., : extent + offset], widths + [(-offset, 0)])


def encode(values):
    top = jnp.maximum(jnp.max(jnp.abs(values), axis=0, keepdims=True) * 1.01, LEAST)
    top = lax.reduce_precision(top, 8, 7)
    factor = (2 * SPAN) / top
    code = jnp.exp2(jnp.abs(values) * factor - SPAN)
    code = jnp.where(values < 0, -code, code).astype(BF16)
    return jnp.concatenate([code, jnp.broadcast_to(top.astype(BF16), (16, top.shape[1]))], axis=0)


def decode(coded):
    number = coded.shape[0] - 16
    step = coded[number : number + 1].astype(F32) * (0.5 / SPAN)
    code = coded[:number].astype(F32)
    size = (jnp.log2(jnp.abs(code)) + SPAN) * step
    return jnp.where(code < 0, -size, size)


def gathered(x):
    size, me = lax.axis_size("chan"), lax.axis_index("chan")
    blocks = jnp.stack([x] + [exchange(x, "chan", k) for k in range(1, size)])
    bit = 1
    while bit < size:
        pairs = blocks.reshape((-1, 2, bit) + x.shape)
        swapped = jnp.stack([pairs[:, 1], pairs[:, 0]], axis=1)
        blocks = jnp.where((me // bit) % 2 == 1, swapped, pairs).reshape(blocks.shape)
        bit *= 2
    return blocks.reshape((size * x.shape[0],) + x.shape[1:])


def per_device(activations, weights, cotangent):
    local, height, width = activations.shape
    chans, rows = lax.axis_size("chan"), lax.axis_size("rows")
    chips, zs = rows // 2, chans // 2
    me, row = lax.axis_index("chan"), lax.axis_index("rows")
    core, chip = row % 2, row // 2
    own_y, own_z = me % 2, me // 2
    first = core == 0
    share = local // rows
    channels = weights.shape[3]
    cells = height * rows * width
    taps = weights.reshape(9, local, channels)

    edges = [(i, i + 1) for i in range(1, rows - 1, 2)]
    edge = jnp.where(first, cotangent[:, 0], cotangent[:, height - 1])
    halo = lax.ppermute(edge, "rows", edges + [(j, i) for i, j in edges])
    mine = jnp.concatenate([cotangent, halo[:, None]], axis=1)
    other = exchange(mine, "rows", 1)
    low, high = jnp.where(first, mine, other), jnp.where(first, other, mine)
    slab = jnp.concatenate([low[:, height:], low[:, :height], high], axis=1)

    xs = gathered(activations.reshape(local, height * width))
    xo = exchange(xs, "rows", 1)
    xchip = jnp.concatenate([jnp.where(first, xs, xo), jnp.where(first, xo, xs)], axis=1)

    window = jnp.where(first, slab[:, : height + 2], slab[:, height:])
    shifted = [shift_columns(window, 1 - b) for b in range(3)]
    stack = jnp.concatenate(
        [shifted[b][:, 2 - a : 2 - a + height].reshape(local, -1) for a in range(3) for b in range(3)], axis=0
    )
    partial = lax.dot_general(
        stack, taps.reshape(9 * local, channels), (((0,), (0,)), ((), ())), preferred_element_type=F32
    )
    pairs = partial.reshape(height * width, zs, 2, local)
    keep = jnp.where(own_y == 0, pairs[:, :, 0], pairs[:, :, 1]).reshape(height * width, zs * local)
    give = jnp.where(own_y == 0, pairs[:, :, 1], pairs[:, :, 0]).reshape(height * width, zs * local)
    total = keep + decode(exchange(encode(give), "chan", 1))
    coded = encode(total)
    grad = lax.dynamic_slice_in_dim(total, own_z * local, local, axis=1)
    for k in range(1, zs):
        piece = lax.dynamic_slice_in_dim(coded, (own_z ^ k) * local, local, axis=1)
        grad = grad + decode(exchange(piece, "chan", 2 * k))
    input_grad = grad.T.reshape(local, height, width).astype(BF16)

    def half(x, axis):
        shape = x.shape[:axis] + (chips, 2, share) + x.shape[axis + 1 :]
        x = x.reshape(shape)
        return jnp.where(first, lax.index_in_dim(x, 0, axis + 1, False), lax.index_in_dim(x, 1, axis + 1, False))

    gs = half(slab, 0)
    moved = [shift_columns(gs, 1 - b) for b in range(3)]
    lines = jnp.stack(
        [moved[b][:, :, 2 - a : 2 - a + 2 * height].reshape(chips, share, -1) for a in range(3) for b in range(3)],
        axis=1,
    )
    sums = lax.dot_general(
        lines.reshape(chips * 9 * share, -1), xchip, (((1,), (1,)), ((), ())), preferred_element_type=F32
    ).reshape(chips, 9 * share, channels)
    filter_sum = lax.dynamic_index_in_dim(sums, chip, 0, False)
    for k in range(1, chips):
        piece = encode(lax.dynamic_index_in_dim(sums, chip ^ k, 0, False))
        filter_sum = filter_sum + decode(exchange(piece, "rows", 2 * k))
    filter_grad = (filter_sum * (1.0 / math.sqrt(cells))).reshape(3, 3, share, channels)

    wh = half(taps, 1).reshape(9 * chips * share, channels)
    parts = lax.dot_general(wh, xchip, (((1,), (0,)), ((), ())), preferred_element_type=F32)
    parts = parts.reshape(3, 3, chips * share, 2 * height, width)
    line = sum(shift_columns(
        sum(jnp.pad(parts[a, b], ((0, 0), (2 - a, a), (0, 0))) for a in range(3)), b - 1) for b in range(3))
    up = [(i, i + 2) for i in range(rows - 2)]
    above = lax.ppermute(line[:, -1], "rows", up)
    below = lax.ppermute(line[:, 0], "rows", [(j, i) for i, j in up])
    inner = line[:, 1:-1]
    inner = inner.at[:, 0].add(above).at[:, -1].add(below).astype(BF16)
    stay = jnp.where(first, inner[:, :height], inner[:, height:])
    go = jnp.where(first, inner[:, height:], inner[:, :height])
    come = exchange(go, "rows", 1)
    stay, come = (x.reshape(chips, share, height, width) for x in (stay, come))
    output = jnp.stack([jnp.where(first, stay, come), jnp.where(first, come, stay)], axis=1)
    return output.reshape(local, height, width), input_grad, filter_grad


def solution(mesh):
    placed = (P("chan", "rows", None), P(None, None, "chan", None), P("chan", "rows", None))
    return jax.shard_map(
        per_device,
        mesh=mesh,
        in_specs=placed,
        out_specs=(
            P("chan", "rows", None),
            P("chan", "rows", None),
            P(None, None, ("chan", "rows"), None),
        ),
        check_vma=False,
    )
```

```python
import functools
import math

import jax
import jax.numpy as jnp
from jax import lax
from jax.experimental import pallas as pl
from jax.experimental.pallas import tpu as pltpu
from jax.sharding import PartitionSpec as P

BF16, F32 = jnp.bfloat16, jnp.float32
SPAN = 124.0
LEAST = 2.0**-100
EXTRA = 16
VMEM_BYTES = 40 * 2**20


def call(body, outs, args, scratch=(), flops=0):
    size = sum(math.prod(x.shape) * x.dtype.itemsize for x in (*outs, *args))
    return pl.pallas_call(
        body,
        out_shape=tuple(outs),
        in_specs=[pl.BlockSpec(memory_space=pltpu.VMEM)] * len(args),
        out_specs=tuple(pl.BlockSpec(memory_space=pltpu.VMEM) for _ in outs),
        scratch_shapes=list(scratch),
        compiler_params=pltpu.CompilerParams(vmem_limit_bytes=VMEM_BYTES),
        cost_estimate=pl.CostEstimate(flops=flops, bytes_accessed=size, transcendentals=0),
    )(*args)


def shape(dims, dtype):
    return jax.ShapeDtypeStruct(dims, dtype)


def rounded_up(top):
    return jnp.maximum(top * 1.01, LEAST).astype(BF16)


def put_coded(ref, columns, values):
    number = values.shape[0]
    size = jnp.abs(values)
    top = rounded_up(jnp.max(size, axis=0, keepdims=True))
    code = jnp.exp2(size * ((2 * SPAN) / top.astype(F32)) - SPAN)
    ref[:number, columns] = jnp.where(values < 0, -code, code).astype(BF16)
    ref[number:, columns] = jnp.broadcast_to(top, (EXTRA, values.shape[1]))


def get_coded(ref, columns):
    number = ref.shape[0] - EXTRA
    step = ref[number:, columns].astype(F32)[:1] * (0.5 / SPAN)
    code = ref[:number, columns].astype(F32)
    size = (jnp.log2(jnp.abs(code)) + SPAN) * step
    return jnp.where(code < 0, -size, size)


def window_of(core, own, adj, halo, width):
    before = jnp.where(core == 0, halo, adj[:, -width:])
    after = jnp.where(core == 0, adj[:, :width], halo)
    return jnp.concatenate([before, own, after], axis=1)


def data_kernel(width, own_ref, adj_ref, halo_ref, w_ref, keep_ref, give_ref, left):
    core = lax.axis_index("rows") % 2
    y = lax.axis_index("chan") % 2
    local, cells = own_ref.shape
    slab = window_of(core, own_ref[...], adj_ref[...], halo_ref[...], width).astype(F32)
    turned = slab.T
    count = turned.shape[0]
    column = lax.broadcasted_iota(jnp.int32, turned.shape, 0) % width
    moved = [
        jnp.where(column == width - 1, 0.0, pltpu.roll(turned, count - 1, 0)),
        turned,
        jnp.where(column == 0, 0.0, pltpu.roll(turned, 1, 0)),
    ]
    moved = [m.astype(BF16) for m in moved]
    for a in range(3):
        for b in range(3):
            tap = 3 * a + b
            left[:, tap * local : (tap + 1) * local] = moved[b][(2 - a) * width : (2 - a) * width + cells]
    for z in range(w_ref.shape[1] // (2 * local)):
        sums = jnp.dot(left[...], w_ref[:, 2 * z * local : 2 * (z + 1) * local], preferred_element_type=F32)
        even, odd = sums[:, :local], sums[:, local:]
        here = slice(z * local, (z + 1) * local)
        keep_ref[:, here] = jnp.where(y == 0, even, odd)
        put_coded(give_ref, here, jnp.where(y == 0, odd, even))


def data_sums(own, adj, halo, taps, width):
    local, cells = own.shape
    channels = taps.shape[1]
    outs = [shape((cells, channels // 2), F32), shape((cells + EXTRA, channels // 2), BF16)]
    return call(
        functools.partial(data_kernel, width), outs, (own, adj, halo, taps),
        [pltpu.VMEM((cells, 9 * local), BF16)], 2 * cells * 9 * local * channels,
    )


def middle_kernel(come_ref, keep_ref, own_ref, *piece_refs):
    z = (lax.axis_index("chan") // 2)
    local = own_ref.shape[1]
    for k in range(len(piece_refs) + 1):
        here = pl.ds(pl.multiple_of((z ^ k) * local, local), local)
        total = keep_ref[:, here] + get_coded(come_ref, here)
        if k == 0:
            own_ref[...] = total
        else:
            put_coded(piece_refs[k - 1], slice(None), total)


def middle(come, keep, local):
    cells, columns = keep.shape
    outs = [shape((cells, local), F32)] + [shape((cells + EXTRA, local), BF16)] * (columns // local - 1)
    return call(middle_kernel, outs, (come, keep))


def last_data_kernel(own_ref, *refs):
    total = own_ref[...]
    for ref in refs[:-1]:
        total = total + get_coded(ref, slice(None))
    refs[-1][...] = total.T.astype(BF16)


def last_data(own, pieces):
    return call(last_data_kernel, [shape(own.shape[::-1], BF16)], (own, *pieces))[0]


def pair_of(y, near, far):
    return jnp.concatenate([jnp.where(y == 0, near, far), jnp.where(y == 0, far, near)], axis=0)


def filter_kernel(pairs, width, own_ref, adj_ref, halo_ref, rim_ref, *refs):
    row = lax.axis_index("rows")
    core, chip = row % 2, row // 2
    y = lax.axis_index("chan") % 2
    near, far, near_o, far_o = (refs[i * pairs : (i + 1) * pairs] for i in range(4))
    keep_ref, give_ref, left = refs[4 * pairs :]
    local, cells = own_ref.shape
    share = keep_ref.shape[0] // 9
    own, adj = own_ref[...], adj_ref[...]
    halo, rim = halo_ref[...], rim_ref[...]
    mine = window_of(core, own, adj, halo, width)
    theirs = window_of(1 - core, adj, own, rim, width)
    both = jnp.concatenate([mine, theirs], axis=1)
    place = lax.broadcasted_iota(jnp.int32, (2 * share, local), 0)
    wanted = jnp.where(place < share, chip * 2 + core, (1 - chip) * 2 + core) * share + place % share
    pick = (lax.broadcasted_iota(jnp.int32, (2 * share, local), 1) == wanted).astype(BF16)
    chosen = jnp.dot(pick, both, preferred_element_type=F32)
    count = chosen.shape[1]
    column = lax.broadcasted_iota(jnp.int32, chosen.shape, 1) % width
    moved = [
        jnp.where(column == width - 1, 0.0, pltpu.roll(chosen, count - 1, 1)),
        chosen,
        jnp.where(column == 0, 0.0, pltpu.roll(chosen, 1, 1)),
    ]
    moved = [m.astype(BF16) for m in moved]
    span = count // 2
    for part in range(2):
        for a in range(3):
            for b in range(3):
                tap = 3 * a + b
                start = part * span + (2 - a) * width
                for q in range(2):
                    left[q * 9 * share + tap * share : q * 9 * share + (tap + 1) * share,
                         part * cells : (part + 1) * cells] = moved[b][q * share : (q + 1) * share, start : start + cells]
    for t in range(pairs):
        right = jnp.concatenate(
            [pair_of(y, near[t][...], far[t][...]), pair_of(y, near_o[t][...], far_o[t][...])], axis=1
        )
        here = slice(t * 2 * local, (t + 1) * 2 * local)
        for q in (1, 0):
            sums = lax.dot_general(
                left[q * 9 * share : (q + 1) * 9 * share], right, (((1,), (1,)), ((), ())), preferred_element_type=F32
            )
            if q:
                put_coded(give_ref, here, sums)
            else:
                keep_ref[:, here] = sums


def filter_sums(own, adj, halo, rim, near, far, near_o, far_o, share, width):
    local, cells = own.shape
    pairs = len(near)
    outs = [shape((9 * share, pairs * 2 * local), F32), shape((9 * share + EXTRA, pairs * 2 * local), BF16)]
    return call(
        functools.partial(filter_kernel, pairs, width), outs, (own, adj, halo, rim, *near, *far, *near_o, *far_o),
        [pltpu.VMEM((18 * share, 2 * cells), BF16)], 2 * 18 * share * 2 * cells * pairs * 2 * local,
    )


def last_filter_kernel(groups, scale, *refs):
    z = lax.axis_index("chan") // 2
    out_ref = refs[-1]
    step = out_ref.shape[1] // sum(groups)
    t = 0
    for i, pairs in enumerate(groups):
        for j in range(pairs):
            here = slice(j * step, (j + 1) * step)
            there = pl.ds(pl.multiple_of((z ^ t) * step, step), step)
            out_ref[:, there] = (refs[2 * i][:, here] + get_coded(refs[2 * i + 1], here)) * scale
            t += 1


def last_filter(groups, parts, channels, scale):
    outs = [shape((parts[0].shape[0], channels), F32)]
    return call(functools.partial(last_filter_kernel, groups, scale), outs, parts)[0]


def output_kernel(pairs, width, w_ref, *refs):
    core = lax.axis_index("rows") % 2
    chan = lax.axis_index("chan")
    y, z = chan % 2, chan // 2
    near, far, near_o, far_o = (refs[i * pairs : (i + 1) * pairs] for i in range(4))
    inner_ref, edge_ref, xs, xo = refs[4 * pairs :]
    local, cells = near[0].shape
    for t in range(pairs):
        there = pl.ds(pl.multiple_of((z ^ t) * 2 * local, 2 * local), 2 * local)
        xs[there, :] = pair_of(y, near[t][...], far[t][...])
        other = pair_of(y, near_o[t][...], far_o[t][...])
        xo[there, :] = jnp.where(core == 0, other[:, :width], other[:, -width:])
    filters = w_ref.shape[1]
    w = w_ref[...].reshape(9 * filters, w_ref.shape[2])
    parts = jnp.dot(w, xs[...], preferred_element_type=F32)
    beside = w_ref[pl.ds(jnp.where(core == 0, 6, 0), 3)].reshape(3 * filters, w_ref.shape[2])
    more = jnp.dot(beside, xo[...], preferred_element_type=F32)
    rows = cells // width
    lines = [[None] * 3 for _ in range(rows + 2)]
    for a in range(3):
        for r in range(rows):
            for b in range(3):
                tap = 3 * a + b
                value = parts[tap * filters : (tap + 1) * filters, r * width : (r + 1) * width]
                line = lines[r - a + 2]
                line[b] = value if line[b] is None else line[b] + value
    for b in range(3):
        value = more[b * filters : (b + 1) * filters]
        lines[rows][b] = lines[rows][b] + jnp.where(core == 0, value, 0.0)
        lines[1][b] = lines[1][b] + jnp.where(core == 0, 0.0, value)
    column = lax.broadcasted_iota(jnp.int32, (filters, width), 1)
    total = []
    for line in lines:
        left = jnp.where(column == 0, 0.0, pltpu.roll(line[0], 1, 1))
        right = jnp.where(column == width - 1, 0.0, pltpu.roll(line[2], width - 1, 1))
        total.append(left + line[1] + right)
    for r in range(rows):
        inner_ref[:, r * width : (r + 1) * width] = total[r + 1]
    edge_ref[...] = jnp.where(core == 0, total[0], total[-1])


def output_sums(taps, near, far, near_o, far_o, width):
    filters, channels = taps.shape[1:]
    cells = near[0].shape[1]
    outs = [shape((filters, cells), F32), shape((filters, width), F32)]
    return call(
        functools.partial(output_kernel, len(near), width), outs, (taps, *near, *far, *near_o, *far_o),
        [pltpu.VMEM((channels, cells), BF16), pltpu.VMEM((channels, width), BF16)],
        2 * 9 * filters * channels * cells * 7 // 6,
    )


def last_output_kernel(width, inner_ref, edge_ref, out_ref):
    core = lax.axis_index("rows") % 2
    edge = edge_ref[...]
    rows = inner_ref.shape[1] // width
    for r in range(rows):
        value = inner_ref[:, r * width : (r + 1) * width]
        if r == 0:
            value = value + jnp.where(core == 0, edge, 0.0)
        if r == rows - 1:
            value = value + jnp.where(core == 0, 0.0, edge)
        out_ref[:, r * width : (r + 1) * width] = value.astype(BF16)


def last_output(inner, edge, width):
    return call(functools.partial(last_output_kernel, width), [shape(inner.shape, BF16)], (inner, edge))[0]


def exchange(x, axis, distance):
    size = lax.axis_size(axis)
    return lax.ppermute(x, axis, [(i, i ^ distance) for i in range(size)])


def shift_columns(values, offset):
    if offset == 0:
        return values
    extent = values.shape[-1]
    widths = [(0, 0)] * (values.ndim - 1)
    if offset > 0:
        return jnp.pad(values[..., offset:], widths + [(0, offset)])
    return jnp.pad(values[..., : extent + offset], widths + [(-offset, 0)])


def encode(values):
    top = jnp.maximum(jnp.max(jnp.abs(values), axis=0, keepdims=True) * 1.01, LEAST)
    top = lax.reduce_precision(top, 8, 7)
    factor = (2 * SPAN) / top
    code = jnp.exp2(jnp.abs(values) * factor - SPAN)
    code = jnp.where(values < 0, -code, code).astype(BF16)
    return jnp.concatenate([code, jnp.broadcast_to(top.astype(BF16), (16, top.shape[1]))], axis=0)


def decode(coded):
    number = coded.shape[0] - 16
    step = coded[number : number + 1].astype(F32) * (0.5 / SPAN)
    code = coded[:number].astype(F32)
    size = (jnp.log2(jnp.abs(code)) + SPAN) * step
    return jnp.where(code < 0, -size, size)


def gathered(x):
    size, me = lax.axis_size("chan"), lax.axis_index("chan")
    blocks = jnp.stack([x] + [exchange(x, "chan", k) for k in range(1, size)])
    bit = 1
    while bit < size:
        pairs = blocks.reshape((-1, 2, bit) + x.shape)
        swapped = jnp.stack([pairs[:, 1], pairs[:, 0]], axis=1)
        blocks = jnp.where((me // bit) % 2 == 1, swapped, pairs).reshape(blocks.shape)
        bit *= 2
    return blocks.reshape((size * x.shape[0],) + x.shape[1:])


def plain(activations, weights, cotangent):
    local, height, width = activations.shape
    chans, rows = lax.axis_size("chan"), lax.axis_size("rows")
    chips, zs = rows // 2, chans // 2
    me, row = lax.axis_index("chan"), lax.axis_index("rows")
    core, chip = row % 2, row // 2
    own_y, own_z = me % 2, me // 2
    first = core == 0
    share = local // rows
    channels = weights.shape[3]
    cells = height * rows * width
    taps = weights.reshape(9, local, channels)

    edges = [(i, i + 1) for i in range(1, rows - 1, 2)]
    edge = jnp.where(first, cotangent[:, 0], cotangent[:, height - 1])
    halo = lax.ppermute(edge, "rows", edges + [(j, i) for i, j in edges])
    mine = jnp.concatenate([cotangent, halo[:, None]], axis=1)
    other = exchange(mine, "rows", 1)
    low, high = jnp.where(first, mine, other), jnp.where(first, other, mine)
    slab = jnp.concatenate([low[:, height:], low[:, :height], high], axis=1)

    xs = gathered(activations.reshape(local, height * width))
    xo = exchange(xs, "rows", 1)
    xchip = jnp.concatenate([jnp.where(first, xs, xo), jnp.where(first, xo, xs)], axis=1)

    window = jnp.where(first, slab[:, : height + 2], slab[:, height:])
    shifted = [shift_columns(window, 1 - b) for b in range(3)]
    stack = jnp.concatenate(
        [shifted[b][:, 2 - a : 2 - a + height].reshape(local, -1) for a in range(3) for b in range(3)], axis=0
    )
    partial = lax.dot_general(
        stack, taps.reshape(9 * local, channels), (((0,), (0,)), ((), ())), preferred_element_type=F32
    )
    pairs = partial.reshape(height * width, zs, 2, local)
    keep = jnp.where(own_y == 0, pairs[:, :, 0], pairs[:, :, 1]).reshape(height * width, zs * local)
    give = jnp.where(own_y == 0, pairs[:, :, 1], pairs[:, :, 0]).reshape(height * width, zs * local)
    total = keep + decode(exchange(encode(give), "chan", 1))
    coded = encode(total)
    grad = lax.dynamic_slice_in_dim(total, own_z * local, local, axis=1)
    for k in range(1, zs):
        piece = lax.dynamic_slice_in_dim(coded, (own_z ^ k) * local, local, axis=1)
        grad = grad + decode(exchange(piece, "chan", 2 * k))
    input_grad = grad.T.reshape(local, height, width).astype(BF16)

    def half(x, axis):
        shape = x.shape[:axis] + (chips, 2, share) + x.shape[axis + 1 :]
        x = x.reshape(shape)
        return jnp.where(first, lax.index_in_dim(x, 0, axis + 1, False), lax.index_in_dim(x, 1, axis + 1, False))

    gs = half(slab, 0)
    moved = [shift_columns(gs, 1 - b) for b in range(3)]
    lines = jnp.stack(
        [moved[b][:, :, 2 - a : 2 - a + 2 * height].reshape(chips, share, -1) for a in range(3) for b in range(3)],
        axis=1,
    )
    sums = lax.dot_general(
        lines.reshape(chips * 9 * share, -1), xchip, (((1,), (1,)), ((), ())), preferred_element_type=F32
    ).reshape(chips, 9 * share, channels)
    filter_sum = lax.dynamic_index_in_dim(sums, chip, 0, False)
    for k in range(1, chips):
        piece = encode(lax.dynamic_index_in_dim(sums, chip ^ k, 0, False))
        filter_sum = filter_sum + decode(exchange(piece, "rows", 2 * k))
    filter_grad = (filter_sum * (1.0 / math.sqrt(cells))).reshape(3, 3, share, channels)

    wh = half(taps, 1).reshape(9 * chips * share, channels)
    parts = lax.dot_general(wh, xchip, (((1,), (0,)), ((), ())), preferred_element_type=F32)
    parts = parts.reshape(3, 3, chips * share, 2 * height, width)
    line = sum(shift_columns(
        sum(jnp.pad(parts[a, b], ((0, 0), (2 - a, a), (0, 0))) for a in range(3)), b - 1) for b in range(3))
    up = [(i, i + 2) for i in range(rows - 2)]
    above = lax.ppermute(line[:, -1], "rows", up)
    below = lax.ppermute(line[:, 0], "rows", [(j, i) for i, j in up])
    inner = line[:, 1:-1]
    inner = inner.at[:, 0].add(above).at[:, -1].add(below).astype(BF16)
    stay = jnp.where(first, inner[:, :height], inner[:, height:])
    go = jnp.where(first, inner[:, height:], inner[:, :height])
    come = exchange(go, "rows", 1)
    stay, come = (x.reshape(chips, share, height, width) for x in (stay, come))
    output = jnp.stack([jnp.where(first, stay, come), jnp.where(first, come, stay)], axis=1)
    return output.reshape(local, height, width), input_grad, filter_grad


def fast(activations, weights, cotangent):
    local, height, width = activations.shape
    chans, rows = lax.axis_size("chan"), lax.axis_size("rows")
    zs, share, channels = chans // 2, local // rows, weights.shape[3]
    first = lax.axis_index("rows") % 2 == 0
    taps = weights.reshape(9, local, channels)

    edges = [(i, i + 1) for i in range(1, rows - 1, 2)]
    edges += [(j, i) for i, j in edges]
    edge = jnp.where(first, cotangent[:, 0], cotangent[:, height - 1])
    halo = lax.ppermute(edge, "rows", edges)
    g = cotangent.reshape(local, height * width)
    adj = exchange(g, "rows", 1)
    x = activations.reshape(local, height * width)

    keep, give = data_sums(g, adj, halo, taps.reshape(9 * local, channels), width)
    come = exchange(give, "chan", 1)

    blocks = {0: x}
    for k in (6, 4, 2, 7, 5, 3, 1):
        blocks[k] = exchange(x, "chan", k)
    near, far = [blocks[2 * t] for t in range(zs)], [blocks[2 * t + 1] for t in range(zs)]
    near_o, far_o = ([exchange(b, "rows", 1) for b in side] for side in (near, far))
    rim = exchange(halo, "rows", 1)

    groups, parts, start = (zs // 2, zs - zs // 2), [], 0
    for pairs in groups:
        chosen = slice(start, start + pairs)
        mine, gift = filter_sums(
            g, adj, halo, rim, near[chosen], far[chosen], near_o[chosen], far_o[chosen], share, width
        )
        parts += [mine, exchange(gift, "rows", 2)]
        start += pairs

    inner, rest = output_sums(taps, near, far, near_o, far_o, width)
    output = last_output(inner, lax.ppermute(rest, "rows", edges), width)

    own, *pieces = middle(come, keep, local)
    pieces = [exchange(piece, "chan", 2 * k) for k, piece in enumerate(pieces, 1)]
    input_grad = last_data(own, pieces)

    scale = 1.0 / math.sqrt(height * rows * width)
    filter_grad = last_filter(groups, parts, channels, scale)
    return (
        output.reshape(local, height, width),
        input_grad.reshape(local, height, width),
        filter_grad.reshape(3, 3, share, channels),
    )


def per_device(activations, weights, cotangent):
    local, height, width = activations.shape
    rows = lax.axis_size("rows")
    whole_tiles = local % 128 == 0 and width % 128 == 0 and (local // rows) % 16 == 0
    if whole_tiles and height == 2 and rows == 4:
        return fast(activations, weights, cotangent)
    return plain(activations, weights, cotangent)


def solution(mesh):
    placed = (P("chan", "rows", None), P(None, None, "chan", None), P("chan", "rows", None))
    return jax.shard_map(
        per_device,
        mesh=mesh,
        in_specs=placed,
        out_specs=(
            P("chan", "rows", None),
            P("chan", "rows", None),
            P(None, None, ("chan", "rows"), None),
        ),
        check_vma=False,
    )
```

```python
import functools
import math

import jax
import jax.numpy as jnp
from jax import lax
from jax.experimental import pallas as pl
from jax.experimental.pallas import tpu as pltpu
from jax.sharding import PartitionSpec as P

BF16, F32 = jnp.bfloat16, jnp.float32
SPAN = 124.0
LEAST = 2.0**-100
EXTRA = 16
VMEM_BYTES = 40 * 2**20


def call(body, outs, args, scratch=(), flops=0, after=()):
    def step(*refs):
        body(*refs[: len(args)], *refs[len(args) + len(after) :])

    return pl.pallas_call(
        step,
        out_shape=tuple(outs),
        in_specs=[pl.BlockSpec(memory_space=pltpu.VMEM)] * len(args) + [pl.BlockSpec(memory_space=pl.ANY)] * len(after),
        out_specs=tuple(pl.BlockSpec(memory_space=pltpu.VMEM) for _ in outs),
        scratch_shapes=list(scratch),
        compiler_params=pltpu.CompilerParams(vmem_limit_bytes=VMEM_BYTES),
        cost_estimate=pl.CostEstimate(flops=int(flops), bytes_accessed=0, transcendentals=0),
    )(*args, *after)


def shape(dims, dtype):
    return jax.ShapeDtypeStruct(dims, dtype)


def rounded_up(top):
    return jnp.maximum(top * 1.01, LEAST).astype(BF16)


def put_coded(ref, columns, values):
    number = values.shape[0]
    size = jnp.abs(values)
    top = rounded_up(jnp.max(size, axis=0, keepdims=True))
    code = jnp.exp2(size * ((2 * SPAN) / top.astype(F32)) - SPAN)
    ref[:number, columns] = jnp.where(values < 0, -code, code).astype(BF16)
    ref[number:, columns] = jnp.broadcast_to(top, (EXTRA, values.shape[1]))


def get_coded(ref, columns):
    number = ref.shape[0] - EXTRA
    step = ref[number:, columns].astype(F32)[:1] * (0.5 / SPAN)
    code = ref[:number, columns].astype(F32)
    size = (jnp.log2(jnp.abs(code)) + SPAN) * step
    return jnp.where(code < 0, -size, size)


def window_of(core, own, adj, halo, width):
    before = jnp.where(core == 0, halo, adj[:, -width:])
    after = jnp.where(core == 0, adj[:, :width], halo)
    return jnp.concatenate([before, own, after], axis=1)


def data_kernel(width, own_ref, adj_ref, halo_ref, w_ref, keep_ref, give_ref, left):
    core = lax.axis_index("rows") % 2
    y = lax.axis_index("chan") % 2
    local, cells = own_ref.shape
    slab = window_of(core, own_ref[...], adj_ref[...], halo_ref[...], width).astype(F32)
    turned = slab.T
    count = turned.shape[0]
    column = lax.broadcasted_iota(jnp.int32, turned.shape, 0) % width
    moved = [
        jnp.where(column == width - 1, 0.0, pltpu.roll(turned, count - 1, 0)),
        turned,
        jnp.where(column == 0, 0.0, pltpu.roll(turned, 1, 0)),
    ]
    moved = [m.astype(BF16) for m in moved]
    for a in range(3):
        for b in range(3):
            tap = 3 * a + b
            left[:, tap * local : (tap + 1) * local] = moved[b][(2 - a) * width : (2 - a) * width + cells]
    for z in range(w_ref.shape[1] // (2 * local)):
        sums = jnp.dot(left[...], w_ref[:, 2 * z * local : 2 * (z + 1) * local], preferred_element_type=F32)
        even, odd = sums[:, :local], sums[:, local:]
        here = slice(z * local, (z + 1) * local)
        keep_ref[:, here] = jnp.where(y == 0, even, odd)
        put_coded(give_ref, here, jnp.where(y == 0, odd, even))


def data_sums(own, adj, halo, taps, width, cost, after=()):
    local, cells = own.shape
    channels = taps.shape[1]
    outs = [shape((cells, channels // 2), F32), shape((cells + EXTRA, channels // 2), BF16)]
    return call(
        functools.partial(data_kernel, width), outs, (own, adj, halo, taps),
        [pltpu.VMEM((cells, 9 * local), BF16)], cost, after,
    )


def middle_kernel(come_ref, keep_ref, own_ref, *piece_refs):
    z = (lax.axis_index("chan") // 2)
    local = own_ref.shape[1]
    for k in range(len(piece_refs) + 1):
        here = pl.ds(pl.multiple_of((z ^ k) * local, local), local)
        total = keep_ref[:, here] + get_coded(come_ref, here)
        if k == 0:
            own_ref[...] = total
        else:
            put_coded(piece_refs[k - 1], slice(None), total)


def middle(come, keep, local, cost, after=()):
    cells, columns = keep.shape
    outs = [shape((cells, local), F32)] + [shape((cells + EXTRA, local), BF16)] * (columns // local - 1)
    return call(middle_kernel, outs, (come, keep), (), cost, after)


def put_rows(ref, values):
    width = ref.shape[2]
    for r in range(ref.shape[1]):
        ref[:, r, :] = values[:, r * width : (r + 1) * width].astype(BF16)


def last_data_kernel(own_ref, *refs):
    total = own_ref[...]
    for ref in refs[:-1]:
        total = total + get_coded(ref, slice(None))
    put_rows(refs[-1], total.T)


def last_data(own, pieces, height, cost, after=()):
    cells, local = own.shape
    outs = [shape((local, height, cells // height), BF16)]
    return call(last_data_kernel, outs, (own, *pieces), (), cost, after)[0]


def views(blocks):
    arrays, places = [], []
    for array, start in blocks:
        found = [i for i, held in enumerate(arrays) if held is array]
        if not found:
            arrays.append(array)
        places.append((found[0] if found else len(arrays) - 1, start))
    return arrays, places


def pair_of(y, near, far):
    return jnp.concatenate([jnp.where(y == 0, near, far), jnp.where(y == 0, far, near)], axis=0)


def lines_kernel(width, own_ref, adj_ref, halo_ref, rim_ref, left):
    row = lax.axis_index("rows")
    core, chip = row % 2, row // 2
    local, cells = own_ref.shape
    share = left.shape[0] // 18
    own, adj = own_ref[...], adj_ref[...]
    halo, rim = halo_ref[...], rim_ref[...]
    mine = window_of(core, own, adj, halo, width)
    theirs = window_of(1 - core, adj, own, rim, width)
    both = jnp.concatenate([mine, theirs], axis=1)
    place = lax.broadcasted_iota(jnp.int32, (2 * share, local), 0)
    wanted = jnp.where(place < share, chip * 2 + core, (1 - chip) * 2 + core) * share + place % share
    pick = (lax.broadcasted_iota(jnp.int32, (2 * share, local), 1) == wanted).astype(BF16)
    chosen = jnp.dot(pick, both, preferred_element_type=F32)
    count = chosen.shape[1]
    column = lax.broadcasted_iota(jnp.int32, chosen.shape, 1) % width
    moved = [
        jnp.where(column == width - 1, 0.0, pltpu.roll(chosen, count - 1, 1)),
        chosen,
        jnp.where(column == 0, 0.0, pltpu.roll(chosen, 1, 1)),
    ]
    moved = [m.astype(BF16) for m in moved]
    span = count // 2
    for part in range(2):
        for a in range(3):
            for b in range(3):
                tap = 3 * a + b
                start = part * span + (2 - a) * width
                for q in range(2):
                    left[q * 9 * share + tap * share : q * 9 * share + (tap + 1) * share,
                         part * cells : (part + 1) * cells] = moved[b][q * share : (q + 1) * share, start : start + cells]


def filter_lines(own, adj, halo, rim, share, width, cost, after=()):
    cells = own.shape[1]
    outs = [shape((18 * share, 2 * cells), BF16)]
    return call(functools.partial(lines_kernel, width), outs, (own, adj, halo, rim), (), cost, after)[0]


def stack_kernel(*refs):
    start = 0
    for ref in refs[:-1]:
        refs[-1][start : start + ref.shape[0]] = ref[...]
        start += ref.shape[0]


def stacked(blocks, cost, after=()):
    rows, columns = blocks[0].shape
    return call(stack_kernel, [shape((len(blocks) * rows, columns), BF16)], blocks, (), cost, after)[0]


def filter_kernel(places, left, *refs):
    y = lax.axis_index("chan") % 2
    keep_ref, give_ref = refs[-2:]
    share = keep_ref.shape[0] // 9
    pairs = len(places) // 4
    local = keep_ref.shape[1] // (2 * pairs)
    held = [refs[i][start : start + local] for i, start in places]
    near, far, near_o, far_o = (held[i * pairs : (i + 1) * pairs] for i in range(4))
    for t in range(pairs):
        right = jnp.concatenate(
            [pair_of(y, near[t], far[t]), pair_of(y, near_o[t], far_o[t])], axis=1
        )
        here = slice(t * 2 * local, (t + 1) * 2 * local)
        for q in (1, 0):
            sums = lax.dot_general(
                left[q * 9 * share : (q + 1) * 9 * share], right, (((1,), (1,)), ((), ())), preferred_element_type=F32
            )
            if q:
                put_coded(give_ref, here, sums)
            else:
                keep_ref[:, here] = sums


def filter_sums(lines, near, far, near_o, far_o, local, cost, after=()):
    share, pairs = lines.shape[0] // 18, len(near)
    arrays, places = views([*near, *far, *near_o, *far_o])
    outs = [shape((9 * share, pairs * 2 * local), F32), shape((9 * share + EXTRA, pairs * 2 * local), BF16)]
    return call(functools.partial(filter_kernel, places), outs, (lines, *arrays), (), cost, after)


def last_filter_kernel(groups, scale, *refs):
    z = lax.axis_index("chan") // 2
    out_ref = refs[-1]
    step = out_ref.shape[1] // sum(groups)
    t = 0
    for i, pairs in enumerate(groups):
        for j in range(pairs):
            here = slice(j * step, (j + 1) * step)
            there = pl.ds(pl.multiple_of((z ^ t) * step, step), step)
            out_ref[:, there] = (refs[2 * i][:, here] + get_coded(refs[2 * i + 1], here)) * scale
            t += 1


def last_filter(groups, parts, channels, scale, cost, after=()):
    outs = [shape((parts[0].shape[0], channels), F32)]
    return call(functools.partial(last_filter_kernel, groups, scale), outs, parts, (), cost, after)[0]


def output_kernel(places, cells, width, w_ref, *refs):
    core = lax.axis_index("rows") % 2
    chan = lax.axis_index("chan")
    y, z = chan % 2, chan // 2
    inner_ref, edge_ref, xs, xo = refs[-4:]
    pairs = len(places) // 4
    local = w_ref.shape[2] // (2 * pairs)
    held = [refs[i][start : start + local] for i, start in places]
    near, far, near_o, far_o = (held[i * pairs : (i + 1) * pairs] for i in range(4))
    for t in range(pairs):
        there = pl.ds(pl.multiple_of((z ^ t) * 2 * local, 2 * local), 2 * local)
        xs[there, :] = pair_of(y, near[t], far[t])
        other = pair_of(y, near_o[t], far_o[t])
        xo[there, :] = jnp.where(core == 0, other[:, :width], other[:, -width:])
    filters = w_ref.shape[1]
    w = w_ref[...].reshape(9 * filters, w_ref.shape[2])
    parts = jnp.dot(w, xs[...], preferred_element_type=F32)
    beside = w_ref[pl.ds(jnp.where(core == 0, 6, 0), 3)].reshape(3 * filters, w_ref.shape[2])
    more = jnp.dot(beside, xo[...], preferred_element_type=F32)
    rows = cells // width
    lines = [[None] * 3 for _ in range(rows + 2)]
    for a in range(3):
        for r in range(rows):
            for b in range(3):
                tap = 3 * a + b
                value = parts[tap * filters : (tap + 1) * filters, r * width : (r + 1) * width]
                line = lines[r - a + 2]
                line[b] = value if line[b] is None else line[b] + value
    for b in range(3):
        value = more[b * filters : (b + 1) * filters]
        lines[rows][b] = lines[rows][b] + jnp.where(core == 0, value, 0.0)
        lines[1][b] = lines[1][b] + jnp.where(core == 0, 0.0, value)
    column = lax.broadcasted_iota(jnp.int32, (filters, width), 1)
    total = []
    for line in lines:
        left = jnp.where(column == 0, 0.0, pltpu.roll(line[0], 1, 1))
        right = jnp.where(column == width - 1, 0.0, pltpu.roll(line[2], width - 1, 1))
        total.append(left + line[1] + right)
    for r in range(rows):
        inner_ref[:, r * width : (r + 1) * width] = total[r + 1]
    edge_ref[...] = jnp.where(core == 0, total[0], total[-1])


def output_sums(taps, near, far, near_o, far_o, width, cost, after=()):
    filters, channels = taps.shape[1:]
    arrays, places = views([*near, *far, *near_o, *far_o])
    cells = arrays[0].shape[1]
    outs = [shape((filters, cells), F32), shape((filters, width), F32)]
    return call(
        functools.partial(output_kernel, places, cells, width), outs, (taps, *arrays),
        [pltpu.VMEM((channels, cells), BF16), pltpu.VMEM((channels, width), BF16)],
        cost, after,
    )


def last_output_kernel(inner_ref, edge_ref, out_ref):
    core = lax.axis_index("rows") % 2
    edge = edge_ref[...]
    zero = jnp.zeros_like(edge)
    top, bottom = jnp.where(core == 0, edge, zero), jnp.where(core == 0, zero, edge)
    middle_rows = [zero] * (out_ref.shape[1] - 2)
    put_rows(out_ref, inner_ref[...] + jnp.concatenate([top, *middle_rows, bottom], axis=1))


def last_output(inner, edge, cost, after=()):
    filters, width = edge.shape
    outs = [shape((filters, inner.shape[1] // width, width), BF16)]
    return call(last_output_kernel, outs, (inner, edge), (), cost, after)[0]


def exchange(x, axis, distance):
    size = lax.axis_size(axis)
    return lax.ppermute(x, axis, [(i, i ^ distance) for i in range(size)])


def shift_columns(values, offset):
    if offset == 0:
        return values
    extent = values.shape[-1]
    widths = [(0, 0)] * (values.ndim - 1)
    if offset > 0:
        return jnp.pad(values[..., offset:], widths + [(0, offset)])
    return jnp.pad(values[..., : extent + offset], widths + [(-offset, 0)])


def encode(values):
    top = jnp.maximum(jnp.max(jnp.abs(values), axis=0, keepdims=True) * 1.01, LEAST)
    top = lax.reduce_precision(top, 8, 7)
    factor = (2 * SPAN) / top
    code = jnp.exp2(jnp.abs(values) * factor - SPAN)
    code = jnp.where(values < 0, -code, code).astype(BF16)
    return jnp.concatenate([code, jnp.broadcast_to(top.astype(BF16), (16, top.shape[1]))], axis=0)


def decode(coded):
    number = coded.shape[0] - 16
    step = coded[number : number + 1].astype(F32) * (0.5 / SPAN)
    code = coded[:number].astype(F32)
    size = (jnp.log2(jnp.abs(code)) + SPAN) * step
    return jnp.where(code < 0, -size, size)


def gathered(x):
    size, me = lax.axis_size("chan"), lax.axis_index("chan")
    blocks = jnp.stack([x] + [exchange(x, "chan", k) for k in range(1, size)])
    bit = 1
    while bit < size:
        pairs = blocks.reshape((-1, 2, bit) + x.shape)
        swapped = jnp.stack([pairs[:, 1], pairs[:, 0]], axis=1)
        blocks = jnp.where((me // bit) % 2 == 1, swapped, pairs).reshape(blocks.shape)
        bit *= 2
    return blocks.reshape((size * x.shape[0],) + x.shape[1:])


def plain(activations, weights, cotangent):
    local, height, width = activations.shape
    chans, rows = lax.axis_size("chan"), lax.axis_size("rows")
    chips, zs = rows // 2, chans // 2
    me, row = lax.axis_index("chan"), lax.axis_index("rows")
    core, chip = row % 2, row // 2
    own_y, own_z = me % 2, me // 2
    first = core == 0
    share = local // rows
    channels = weights.shape[3]
    cells = height * rows * width
    taps = weights.reshape(9, local, channels)

    edges = [(i, i + 1) for i in range(1, rows - 1, 2)]
    edge = jnp.where(first, cotangent[:, 0], cotangent[:, height - 1])
    halo = lax.ppermute(edge, "rows", edges + [(j, i) for i, j in edges])
    mine = jnp.concatenate([cotangent, halo[:, None]], axis=1)
    other = exchange(mine, "rows", 1)
    low, high = jnp.where(first, mine, other), jnp.where(first, other, mine)
    slab = jnp.concatenate([low[:, height:], low[:, :height], high], axis=1)

    xs = gathered(activations.reshape(local, height * width))
    xo = exchange(xs, "rows", 1)
    xchip = jnp.concatenate([jnp.where(first, xs, xo), jnp.where(first, xo, xs)], axis=1)

    window = jnp.where(first, slab[:, : height + 2], slab[:, height:])
    shifted = [shift_columns(window, 1 - b) for b in range(3)]
    stack = jnp.concatenate(
        [shifted[b][:, 2 - a : 2 - a + height].reshape(local, -1) for a in range(3) for b in range(3)], axis=0
    )
    partial = lax.dot_general(
        stack, taps.reshape(9 * local, channels), (((0,), (0,)), ((), ())), preferred_element_type=F32
    )
    pairs = partial.reshape(height * width, zs, 2, local)
    keep = jnp.where(own_y == 0, pairs[:, :, 0], pairs[:, :, 1]).reshape(height * width, zs * local)
    give = jnp.where(own_y == 0, pairs[:, :, 1], pairs[:, :, 0]).reshape(height * width, zs * local)
    total = keep + decode(exchange(encode(give), "chan", 1))
    coded = encode(total)
    grad = lax.dynamic_slice_in_dim(total, own_z * local, local, axis=1)
    for k in range(1, zs):
        piece = lax.dynamic_slice_in_dim(coded, (own_z ^ k) * local, local, axis=1)
        grad = grad + decode(exchange(piece, "chan", 2 * k))
    input_grad = grad.T.reshape(local, height, width).astype(BF16)

    def half(x, axis):
        shape = x.shape[:axis] + (chips, 2, share) + x.shape[axis + 1 :]
        x = x.reshape(shape)
        return jnp.where(first, lax.index_in_dim(x, 0, axis + 1, False), lax.index_in_dim(x, 1, axis + 1, False))

    gs = half(slab, 0)
    moved = [shift_columns(gs, 1 - b) for b in range(3)]
    lines = jnp.stack(
        [moved[b][:, :, 2 - a : 2 - a + 2 * height].reshape(chips, share, -1) for a in range(3) for b in range(3)],
        axis=1,
    )
    sums = lax.dot_general(
        lines.reshape(chips * 9 * share, -1), xchip, (((1,), (1,)), ((), ())), preferred_element_type=F32
    ).reshape(chips, 9 * share, channels)
    filter_sum = lax.dynamic_index_in_dim(sums, chip, 0, False)
    for k in range(1, chips):
        piece = encode(lax.dynamic_index_in_dim(sums, chip ^ k, 0, False))
        filter_sum = filter_sum + decode(exchange(piece, "rows", 2 * k))
    filter_grad = (filter_sum * (1.0 / math.sqrt(cells))).reshape(3, 3, share, channels)

    wh = half(taps, 1).reshape(9 * chips * share, channels)
    parts = lax.dot_general(wh, xchip, (((1,), (0,)), ((), ())), preferred_element_type=F32)
    parts = parts.reshape(3, 3, chips * share, 2 * height, width)
    line = sum(shift_columns(
        sum(jnp.pad(parts[a, b], ((0, 0), (2 - a, a), (0, 0))) for a in range(3)), b - 1) for b in range(3))
    up = [(i, i + 2) for i in range(rows - 2)]
    above = lax.ppermute(line[:, -1], "rows", up)
    below = lax.ppermute(line[:, 0], "rows", [(j, i) for i, j in up])
    inner = line[:, 1:-1]
    inner = inner.at[:, 0].add(above).at[:, -1].add(below).astype(BF16)
    stay = jnp.where(first, inner[:, :height], inner[:, height:])
    go = jnp.where(first, inner[:, height:], inner[:, :height])
    come = exchange(go, "rows", 1)
    stay, come = (x.reshape(chips, share, height, width) for x in (stay, come))
    output = jnp.stack([jnp.where(first, stay, come), jnp.where(first, come, stay)], axis=1)
    return output.reshape(local, height, width), input_grad, filter_grad


def fast(activations, weights, cotangent):
    local, height, width = activations.shape
    chans, rows = lax.axis_size("chan"), lax.axis_size("rows")
    zs, share, channels = chans // 2, local // rows, weights.shape[3]
    first = lax.axis_index("rows") % 2 == 0
    taps = weights.reshape(9, local, channels)

    edges = [(i, i + 1) for i in range(1, rows - 1, 2)]
    edges += [(j, i) for i, j in edges]
    g = cotangent.reshape(local, height * width)
    edge = jnp.where(first, g[:, :width], g[:, -width:])
    halo = lax.ppermute(edge, "rows", edges)
    adj = exchange(g, "rows", 1)
    x = activations.reshape(local, height * width)

    half = zs // 2
    direct = {0: x}
    for k in (1, 3, 2, 6, 4):
        direct[k] = exchange(x, "chan", k)

    keep, give = data_sums(g, adj, halo, taps.reshape(9 * local, channels), width, 24000000000.0)
    come = exchange(give, "chan", 1)

    others = {k: exchange(direct[k], "rows", 1) for k in range(2 * half)}
    rim = exchange(halo, "rows", 1)
    rim, give = lax.optimization_barrier((rim, give))
    lines = filter_lines(g, adj, halo, rim, share, width, 12000000000.0)
    near = [(direct[2 * t], 0) for t in range(half)]
    far = [(direct[2 * t + 1], 0) for t in range(half)]
    near_o = [(others[2 * t], 0) for t in range(half)]
    far_o = [(others[2 * t + 1], 0) for t in range(half)]
    mine, gift = filter_sums(lines, near, far, near_o, far_o, local, 0)
    far_z = jnp.concatenate([direct[2 * t] for t in range(half, zs)], axis=0)
    far_z, give = lax.optimization_barrier((far_z, give))
    far_zy = exchange(far_z, "chan", 1)
    far_zo, far_zyo = exchange(far_z, "rows", 1), exchange(far_zy, "rows", 1)
    near2 = [(far_z, t * local) for t in range(zs - half)]
    far2 = [(far_zy, t * local) for t in range(zs - half)]
    near2_o = [(far_zo, t * local) for t in range(zs - half)]
    far2_o = [(far_zyo, t * local) for t in range(zs - half)]
    own, *pieces = middle(come, keep, local, 0)
    pieces = [exchange(piece, "chan", 2 * k) for k, piece in enumerate(pieces, 1)]
    mine2, gift2 = filter_sums(lines, near2, far2, near2_o, far2_o, local, 0)
    parts = [mine, exchange(gift, "rows", 2), mine2, exchange(gift2, "rows", 2)]
    groups = (half, zs - half)
    inner, rest = output_sums(taps, near + near2, far + far2, near_o + near2_o, far_o + far2_o, width, 0)
    output = last_output(inner, lax.ppermute(rest, "rows", edges), 0)

    scale = 1.0 / math.sqrt(height * rows * width)
    filter_grad = last_filter(groups, parts, channels, scale, 0)
    input_grad = last_data(own, pieces, height, 0, (filter_grad,))
    return (
        output,
        input_grad,
        filter_grad.reshape(3, 3, share, channels),
    )


def per_device(activations, weights, cotangent):
    local, height, width = activations.shape
    rows = lax.axis_size("rows")
    whole_tiles = local % 128 == 0 and width % 128 == 0 and (local // rows) % 16 == 0
    if whole_tiles and height == 2 and rows == 4:
        return fast(activations, weights, cotangent)
    return plain(activations, weights, cotangent)


def solution(mesh):
    placed = (P("chan", "rows", None), P(None, None, "chan", None), P("chan", "rows", None))
    return jax.shard_map(
        per_device,
        mesh=mesh,
        in_specs=placed,
        out_specs=(
            P("chan", "rows", None),
            P("chan", "rows", None),
            P(None, None, ("chan", "rows"), None),
        ),
        check_vma=False,
    )
```

```python
import functools
import math

import jax
import jax.numpy as jnp
from jax import lax
from jax.experimental import pallas as pl
from jax.experimental.pallas import tpu as pltpu
from jax.sharding import PartitionSpec as P

BF16, F32 = jnp.bfloat16, jnp.float32
SPAN = 124.0
LEAST = 2.0**-100
EXTRA = 16
VMEM_BYTES = 40 * 2**20


def call(body, outs, args, scratch=(), flops=0, after=(), far_out=()):
    def step(*refs):
        body(*refs[: len(args)], *refs[len(args) + len(after) :])

    return pl.pallas_call(
        step,
        out_shape=tuple(outs),
        in_specs=[pl.BlockSpec(memory_space=pltpu.VMEM)] * len(args)
        + [pl.BlockSpec(memory_space=pl.ANY)] * len(after),
        out_specs=tuple(pl.BlockSpec(memory_space=pltpu.HBM if i in far_out else pltpu.VMEM) for i in range(len(outs))),
        scratch_shapes=list(scratch),
        compiler_params=pltpu.CompilerParams(vmem_limit_bytes=VMEM_BYTES),
        cost_estimate=pl.CostEstimate(flops=int(flops), bytes_accessed=0, transcendentals=0),
    )(*args, *after)


def shape(dims, dtype):
    return jax.ShapeDtypeStruct(dims, dtype)


def rounded_up(top):
    return jnp.maximum(top * 1.01, LEAST).astype(BF16)


def put_coded(ref, columns, values):
    number = values.shape[0]
    size = jnp.abs(values)
    top = rounded_up(jnp.max(size, axis=0, keepdims=True))
    code = jnp.exp2(size * ((2 * SPAN) / top.astype(F32)) - SPAN)
    ref[:number, columns] = jnp.where(values < 0, -code, code).astype(BF16)
    ref[number:, columns] = jnp.broadcast_to(top, (EXTRA, values.shape[1]))


def get_coded(ref, columns, rows=None):
    number = ref.shape[0] - EXTRA
    rows = slice(0, number) if rows is None else rows
    step = ref[number:, columns].astype(F32)[:1] * (0.5 / SPAN)
    code = ref[rows, columns].astype(F32)
    size = (jnp.log2(jnp.abs(code)) + SPAN) * step
    return jnp.where(code < 0, -size, size)


def window_of(core, own, adj, halo, width):
    before = jnp.where(core == 0, halo, adj[:, -width:])
    after = jnp.where(core == 0, adj[:, :width], halo)
    return jnp.concatenate([before, own, after], axis=1)


def data_kernel(width, own_ref, adj_ref, halo_ref, w_ref, keep_ref, give_ref, left):
    core = lax.axis_index("rows") % 2
    y = lax.axis_index("chan") % 2
    local, cells = own_ref.shape
    slab = window_of(core, own_ref[...], adj_ref[...], halo_ref[...], width).astype(F32)
    turned = slab.T
    count = turned.shape[0]
    column = lax.broadcasted_iota(jnp.int32, turned.shape, 0) % width
    moved = [
        jnp.where(column == width - 1, 0.0, pltpu.roll(turned, count - 1, 0)),
        turned,
        jnp.where(column == 0, 0.0, pltpu.roll(turned, 1, 0)),
    ]
    moved = [m.astype(BF16) for m in moved]
    for a in range(3):
        for b in range(3):
            tap = 3 * a + b
            left[:, tap * local : (tap + 1) * local] = moved[b][(2 - a) * width : (2 - a) * width + cells]
    for z in range(w_ref.shape[1] // (2 * local)):
        sums = jnp.dot(left[...], w_ref[:, 2 * z * local : 2 * (z + 1) * local], preferred_element_type=F32)
        even, odd = sums[:, :local], sums[:, local:]
        here = slice(z * local, (z + 1) * local)
        keep_ref[:, here] = jnp.where(y == 0, even, odd)
        put_coded(give_ref, here, jnp.where(y == 0, odd, even))


def data_sums(own, adj, halo, taps, width, cost, after=()):
    local, cells = own.shape
    channels = taps.shape[1]
    outs = [shape((cells, channels // 2), F32), shape((cells + EXTRA, channels // 2), BF16)]
    return call(
        functools.partial(data_kernel, width), outs, (own, adj, halo, taps),
        [pltpu.VMEM((cells, 9 * local), BF16)], cost, after,
    )


def middle_kernel(come_ref, keep_ref, own_ref, *piece_refs):
    z = (lax.axis_index("chan") // 2)
    local = own_ref.shape[1]
    for k in range(len(piece_refs) + 1):
        here = pl.ds(pl.multiple_of((z ^ k) * local, local), local)
        total = keep_ref[:, here] + get_coded(come_ref, here)
        if k == 0:
            own_ref[...] = total
        else:
            put_coded(piece_refs[k - 1], slice(None), total)


def middle(come, keep, local, cost, after=()):
    cells, columns = keep.shape
    outs = [shape((cells, local), F32)] + [shape((cells + EXTRA, local), BF16)] * (columns // local - 1)
    return call(middle_kernel, outs, (come, keep), (), cost, after)


def put_rows(ref, values):
    width = ref.shape[2]
    for r in range(ref.shape[1]):
        ref[:, r, :] = values[:, r * width : (r + 1) * width].astype(BF16)


def last_data_kernel(own_ref, *refs):
    total = own_ref[...]
    for ref in refs[:-1]:
        total = total + get_coded(ref, slice(None))
    put_rows(refs[-1], total.T)


def last_data(own, pieces, height, cost, after=()):
    cells, local = own.shape
    outs = [shape((local, height, cells // height), BF16)]
    return call(last_data_kernel, outs, (own, *pieces), (), cost, after)[0]


def views(blocks):
    arrays, places = [], []
    for array, start in blocks:
        found = [i for i, held in enumerate(arrays) if held is array]
        if not found:
            arrays.append(array)
        places.append((found[0] if found else len(arrays) - 1, start))
    return arrays, places


def pair_of(y, near, far):
    return jnp.concatenate([jnp.where(y == 0, near, far), jnp.where(y == 0, far, near)], axis=0)


def lines_kernel(width, own_ref, adj_ref, halo_ref, rim_ref, left):
    row = lax.axis_index("rows")
    core, chip = row % 2, row // 2
    local, cells = own_ref.shape
    share = left.shape[0] // 18
    own, adj = own_ref[...], adj_ref[...]
    halo, rim = halo_ref[...], rim_ref[...]
    mine = window_of(core, own, adj, halo, width)
    theirs = window_of(1 - core, adj, own, rim, width)
    both = jnp.concatenate([mine, theirs], axis=1)
    place = lax.broadcasted_iota(jnp.int32, (2 * share, local), 0)
    wanted = jnp.where(place < share, chip * 2 + core, (1 - chip) * 2 + core) * share + place % share
    pick = (lax.broadcasted_iota(jnp.int32, (2 * share, local), 1) == wanted).astype(BF16)
    chosen = jnp.dot(pick, both, preferred_element_type=F32)
    count = chosen.shape[1]
    column = lax.broadcasted_iota(jnp.int32, chosen.shape, 1) % width
    moved = [
        jnp.where(column == width - 1, 0.0, pltpu.roll(chosen, count - 1, 1)),
        chosen,
        jnp.where(column == 0, 0.0, pltpu.roll(chosen, 1, 1)),
    ]
    moved = [m.astype(BF16) for m in moved]
    span = count // 2
    for part in range(2):
        for a in range(3):
            for b in range(3):
                tap = 3 * a + b
                start = part * span + (2 - a) * width
                for q in range(2):
                    left[q * 9 * share + tap * share : q * 9 * share + (tap + 1) * share,
                         part * cells : (part + 1) * cells] = moved[b][q * share : (q + 1) * share, start : start + cells]


def filter_lines(own, adj, halo, rim, share, width, cost, after=()):
    cells = own.shape[1]
    outs = [shape((18 * share, 2 * cells), BF16)]
    return call(functools.partial(lines_kernel, width), outs, (own, adj, halo, rim), (), cost, after)[0]


def stack_kernel(*refs):
    start = 0
    for ref in refs[:-1]:
        refs[-1][start : start + ref.shape[0]] = ref[...]
        start += ref.shape[0]


def stacked(blocks, cost, after=()):
    rows, columns = blocks[0].shape
    return call(stack_kernel, [shape((len(blocks) * rows, columns), BF16)], blocks, (), cost, after)[0]


def filter_kernel(places, left, *refs):
    y = lax.axis_index("chan") % 2
    keep_ref, give_ref = refs[-2:]
    share = keep_ref.shape[0] // 9
    pairs = len(places) // 4
    local = keep_ref.shape[1] // (2 * pairs)
    held = [refs[i][start : start + local] for i, start in places]
    near, far, near_o, far_o = (held[i * pairs : (i + 1) * pairs] for i in range(4))
    for t in range(pairs):
        right = jnp.concatenate(
            [pair_of(y, near[t], far[t]), pair_of(y, near_o[t], far_o[t])], axis=1
        )
        here = slice(t * 2 * local, (t + 1) * 2 * local)
        for q in (1, 0):
            sums = lax.dot_general(
                left[q * 9 * share : (q + 1) * 9 * share], right, (((1,), (1,)), ((), ())), preferred_element_type=F32
            )
            if q:
                put_coded(give_ref, here, sums)
            else:
                keep_ref[:, here] = sums


def filter_sums(lines, near, far, near_o, far_o, local, cost, after=()):
    share, pairs = lines.shape[0] // 18, len(near)
    arrays, places = views([*near, *far, *near_o, *far_o])
    outs = [shape((9 * share, pairs * 2 * local), F32), shape((9 * share + EXTRA, pairs * 2 * local), BF16)]
    return call(functools.partial(filter_kernel, places), outs, (lines, *arrays), (), cost, after)


def last_filter_kernel(groups, scale, *refs):
    z = lax.axis_index("chan") // 2
    out_far, sign_ref, done_ref, sent = refs[-4:]
    sign_ref[...] = jnp.zeros_like(sign_ref)
    step = done_ref.shape[1] // sum(groups)
    lines = done_ref.shape[0] // 3
    copies = []
    for a in range(3):
        rows = slice(a * lines, (a + 1) * lines)
        t = 0
        for i, pairs in enumerate(groups):
            for j in range(pairs):
                here = slice(j * step, (j + 1) * step)
                there = pl.ds(pl.multiple_of((z ^ t) * step, step), step)
                done_ref[rows, there] = (refs[2 * i][rows, here] + get_coded(refs[2 * i + 1], here, rows)) * scale
                t += 1
        copies.append(pltpu.make_async_copy(done_ref.at[rows], out_far.at[rows], sent.at[a]))
        copies[-1].start()
    for copy in copies:
        copy.wait()


def last_filter(groups, parts, channels, scale, cost, after=()):
    size = (parts[0].shape[0], channels)
    scratch = [pltpu.VMEM(size, F32), pltpu.SemaphoreType.DMA((3,))]
    kernel = functools.partial(last_filter_kernel, groups, scale)
    return call(kernel, [shape(size, F32), shape((8, 128), F32)], parts, scratch, cost, after, far_out=(0,))


def output_kernel(places, cells, width, w_ref, *refs):
    core = lax.axis_index("rows") % 2
    chan = lax.axis_index("chan")
    y, z = chan % 2, chan // 2
    inner_ref, edge_ref, xs, xo = refs[-4:]
    pairs = len(places) // 4
    local = w_ref.shape[2] // (2 * pairs)
    held = [refs[i][start : start + local] for i, start in places]
    near, far, near_o, far_o = (held[i * pairs : (i + 1) * pairs] for i in range(4))
    for t in range(pairs):
        there = pl.ds(pl.multiple_of((z ^ t) * 2 * local, 2 * local), 2 * local)
        xs[there, :] = pair_of(y, near[t], far[t])
        other = pair_of(y, near_o[t], far_o[t])
        xo[there, :] = jnp.where(core == 0, other[:, :width], other[:, -width:])
    filters = w_ref.shape[1]
    w = w_ref[...].reshape(9 * filters, w_ref.shape[2])
    parts = jnp.dot(w, xs[...], preferred_element_type=F32)
    beside = w_ref[pl.ds(jnp.where(core == 0, 6, 0), 3)].reshape(3 * filters, w_ref.shape[2])
    more = jnp.dot(beside, xo[...], preferred_element_type=F32)
    rows = cells // width
    lines = [[None] * 3 for _ in range(rows + 2)]
    for a in range(3):
        for r in range(rows):
            for b in range(3):
                tap = 3 * a + b
                value = parts[tap * filters : (tap + 1) * filters, r * width : (r + 1) * width]
                line = lines[r - a + 2]
                line[b] = value if line[b] is None else line[b] + value
    for b in range(3):
        value = more[b * filters : (b + 1) * filters]
        lines[rows][b] = lines[rows][b] + jnp.where(core == 0, value, 0.0)
        lines[1][b] = lines[1][b] + jnp.where(core == 0, 0.0, value)
    column = lax.broadcasted_iota(jnp.int32, (filters, width), 1)
    total = []
    for line in lines:
        left = jnp.where(column == 0, 0.0, pltpu.roll(line[0], 1, 1))
        right = jnp.where(column == width - 1, 0.0, pltpu.roll(line[2], width - 1, 1))
        total.append(left + line[1] + right)
    for r in range(rows):
        inner_ref[:, r * width : (r + 1) * width] = total[r + 1]
    edge_ref[...] = jnp.where(core == 0, total[0], total[-1])


def output_sums(taps, near, far, near_o, far_o, width, cost, after=()):
    filters, channels = taps.shape[1:]
    arrays, places = views([*near, *far, *near_o, *far_o])
    cells = arrays[0].shape[1]
    outs = [shape((filters, cells), F32), shape((filters, width), F32)]
    return call(
        functools.partial(output_kernel, places, cells, width), outs, (taps, *arrays),
        [pltpu.VMEM((channels, cells), BF16), pltpu.VMEM((channels, width), BF16)],
        cost, after,
    )


def last_output_kernel(inner_ref, edge_ref, out_ref):
    core = lax.axis_index("rows") % 2
    edge = edge_ref[...]
    zero = jnp.zeros_like(edge)
    top, bottom = jnp.where(core == 0, edge, zero), jnp.where(core == 0, zero, edge)
    middle_rows = [zero] * (out_ref.shape[1] - 2)
    put_rows(out_ref, inner_ref[...] + jnp.concatenate([top, *middle_rows, bottom], axis=1))


def last_output(inner, edge, cost, after=()):
    filters, width = edge.shape
    outs = [shape((filters, inner.shape[1] // width, width), BF16)]
    return call(last_output_kernel, outs, (inner, edge), (), cost, after)[0]


def exchange(x, axis, distance):
    size = lax.axis_size(axis)
    return lax.ppermute(x, axis, [(i, i ^ distance) for i in range(size)])


def shift_columns(values, offset):
    if offset == 0:
        return values
    extent = values.shape[-1]
    widths = [(0, 0)] * (values.ndim - 1)
    if offset > 0:
        return jnp.pad(values[..., offset:], widths + [(0, offset)])
    return jnp.pad(values[..., : extent + offset], widths + [(-offset, 0)])


def encode(values):
    top = jnp.maximum(jnp.max(jnp.abs(values), axis=0, keepdims=True) * 1.01, LEAST)
    top = lax.reduce_precision(top, 8, 7)
    factor = (2 * SPAN) / top
    code = jnp.exp2(jnp.abs(values) * factor - SPAN)
    code = jnp.where(values < 0, -code, code).astype(BF16)
    return jnp.concatenate([code, jnp.broadcast_to(top.astype(BF16), (16, top.shape[1]))], axis=0)


def decode(coded):
    number = coded.shape[0] - 16
    step = coded[number : number + 1].astype(F32) * (0.5 / SPAN)
    code = coded[:number].astype(F32)
    size = (jnp.log2(jnp.abs(code)) + SPAN) * step
    return jnp.where(code < 0, -size, size)


def gathered(x):
    size, me = lax.axis_size("chan"), lax.axis_index("chan")
    blocks = jnp.stack([x] + [exchange(x, "chan", k) for k in range(1, size)])
    bit = 1
    while bit < size:
        pairs = blocks.reshape((-1, 2, bit) + x.shape)
        swapped = jnp.stack([pairs[:, 1], pairs[:, 0]], axis=1)
        blocks = jnp.where((me // bit) % 2 == 1, swapped, pairs).reshape(blocks.shape)
        bit *= 2
    return blocks.reshape((size * x.shape[0],) + x.shape[1:])


def plain(activations, weights, cotangent):
    local, height, width = activations.shape
    chans, rows = lax.axis_size("chan"), lax.axis_size("rows")
    chips, zs = rows // 2, chans // 2
    me, row = lax.axis_index("chan"), lax.axis_index("rows")
    core, chip = row % 2, row // 2
    own_y, own_z = me % 2, me // 2
    first = core == 0
    share = local // rows
    channels = weights.shape[3]
    cells = height * rows * width
    taps = weights.reshape(9, local, channels)

    edges = [(i, i + 1) for i in range(1, rows - 1, 2)]
    edge = jnp.where(first, cotangent[:, 0], cotangent[:, height - 1])
    halo = lax.ppermute(edge, "rows", edges + [(j, i) for i, j in edges])
    mine = jnp.concatenate([cotangent, halo[:, None]], axis=1)
    other = exchange(mine, "rows", 1)
    low, high = jnp.where(first, mine, other), jnp.where(first, other, mine)
    slab = jnp.concatenate([low[:, height:], low[:, :height], high], axis=1)

    xs = gathered(activations.reshape(local, height * width))
    xo = exchange(xs, "rows", 1)
    xchip = jnp.concatenate([jnp.where(first, xs, xo), jnp.where(first, xo, xs)], axis=1)

    window = jnp.where(first, slab[:, : height + 2], slab[:, height:])
    shifted = [shift_columns(window, 1 - b) for b in range(3)]
    stack = jnp.concatenate(
        [shifted[b][:, 2 - a : 2 - a + height].reshape(local, -1) for a in range(3) for b in range(3)], axis=0
    )
    partial = lax.dot_general(
        stack, taps.reshape(9 * local, channels), (((0,), (0,)), ((), ())), preferred_element_type=F32
    )
    pairs = partial.reshape(height * width, zs, 2, local)
    keep = jnp.where(own_y == 0, pairs[:, :, 0], pairs[:, :, 1]).reshape(height * width, zs * local)
    give = jnp.where(own_y == 0, pairs[:, :, 1], pairs[:, :, 0]).reshape(height * width, zs * local)
    total = keep + decode(exchange(encode(give), "chan", 1))
    coded = encode(total)
    grad = lax.dynamic_slice_in_dim(total, own_z * local, local, axis=1)
    for k in range(1, zs):
        piece = lax.dynamic_slice_in_dim(coded, (own_z ^ k) * local, local, axis=1)
        grad = grad + decode(exchange(piece, "chan", 2 * k))
    input_grad = grad.T.reshape(local, height, width).astype(BF16)

    def half(x, axis):
        shape = x.shape[:axis] + (chips, 2, share) + x.shape[axis + 1 :]
        x = x.reshape(shape)
        return jnp.where(first, lax.index_in_dim(x, 0, axis + 1, False), lax.index_in_dim(x, 1, axis + 1, False))

    gs = half(slab, 0)
    moved = [shift_columns(gs, 1 - b) for b in range(3)]
    lines = jnp.stack(
        [moved[b][:, :, 2 - a : 2 - a + 2 * height].reshape(chips, share, -1) for a in range(3) for b in range(3)],
        axis=1,
    )
    sums = lax.dot_general(
        lines.reshape(chips * 9 * share, -1), xchip, (((1,), (1,)), ((), ())), preferred_element_type=F32
    ).reshape(chips, 9 * share, channels)
    filter_sum = lax.dynamic_index_in_dim(sums, chip, 0, False)
    for k in range(1, chips):
        piece = encode(lax.dynamic_index_in_dim(sums, chip ^ k, 0, False))
        filter_sum = filter_sum + decode(exchange(piece, "rows", 2 * k))
    filter_grad = (filter_sum * (1.0 / math.sqrt(cells))).reshape(3, 3, share, channels)

    wh = half(taps, 1).reshape(9 * chips * share, channels)
    parts = lax.dot_general(wh, xchip, (((1,), (0,)), ((), ())), preferred_element_type=F32)
    parts = parts.reshape(3, 3, chips * share, 2 * height, width)
    line = sum(shift_columns(
        sum(jnp.pad(parts[a, b], ((0, 0), (2 - a, a), (0, 0))) for a in range(3)), b - 1) for b in range(3))
    up = [(i, i + 2) for i in range(rows - 2)]
    above = lax.ppermute(line[:, -1], "rows", up)
    below = lax.ppermute(line[:, 0], "rows", [(j, i) for i, j in up])
    inner = line[:, 1:-1]
    inner = inner.at[:, 0].add(above).at[:, -1].add(below).astype(BF16)
    stay = jnp.where(first, inner[:, :height], inner[:, height:])
    go = jnp.where(first, inner[:, height:], inner[:, :height])
    come = exchange(go, "rows", 1)
    stay, come = (x.reshape(chips, share, height, width) for x in (stay, come))
    output = jnp.stack([jnp.where(first, stay, come), jnp.where(first, come, stay)], axis=1)
    return output.reshape(local, height, width), input_grad, filter_grad


def fast(activations, weights, cotangent):
    local, height, width = activations.shape
    chans, rows = lax.axis_size("chan"), lax.axis_size("rows")
    zs, share, channels = chans // 2, local // rows, weights.shape[3]
    first = lax.axis_index("rows") % 2 == 0
    taps = weights.reshape(9, local, channels)

    edges = [(i, i + 1) for i in range(1, rows - 1, 2)]
    edges += [(j, i) for i, j in edges]
    g = cotangent.reshape(local, height * width)
    edge = jnp.where(first, g[:, :width], g[:, -width:])
    halo = lax.ppermute(edge, "rows", edges)
    adj = exchange(g, "rows", 1)
    x = activations.reshape(local, height * width)

    half = zs // 2
    direct = {0: x}
    for k in (1, 3, 2, 6, 4):
        direct[k] = exchange(x, "chan", k)

    keep, give = data_sums(g, adj, halo, taps.reshape(9 * local, channels), width, 24000000000.0)
    come = exchange(give, "chan", 1)

    others = {k: exchange(direct[k], "rows", 1) for k in range(2 * half)}
    rim = exchange(halo, "rows", 1)
    rim, give = lax.optimization_barrier((rim, give))
    lines = filter_lines(g, adj, halo, rim, share, width, 12000000000.0)
    near = [(direct[2 * t], 0) for t in range(half)]
    far = [(direct[2 * t + 1], 0) for t in range(half)]
    near_o = [(others[2 * t], 0) for t in range(half)]
    far_o = [(others[2 * t + 1], 0) for t in range(half)]
    mine, gift = filter_sums(lines, near, far, near_o, far_o, local, 0)
    far_z = jnp.concatenate([direct[2 * t] for t in range(half, zs)], axis=0)
    far_z, give = lax.optimization_barrier((far_z, give))
    far_zy = exchange(far_z, "chan", 1)
    far_zo, far_zyo = exchange(far_z, "rows", 1), exchange(far_zy, "rows", 1)
    near2 = [(far_z, t * local) for t in range(zs - half)]
    far2 = [(far_zy, t * local) for t in range(zs - half)]
    near2_o = [(far_zo, t * local) for t in range(zs - half)]
    far2_o = [(far_zyo, t * local) for t in range(zs - half)]
    own, *pieces = middle(come, keep, local, 0)
    pieces = [exchange(piece, "chan", 2 * k) for k, piece in enumerate(pieces, 1)]
    mine2, gift2 = filter_sums(lines, near2, far2, near2_o, far2_o, local, 0)
    parts = [mine, exchange(gift, "rows", 2), mine2, exchange(gift2, "rows", 2)]
    groups = (half, zs - half)
    inner, rest = output_sums(taps, near + near2, far + far2, near_o + near2_o, far_o + far2_o, width, 0)
    output = last_output(inner, lax.ppermute(rest, "rows", edges), 0)

    scale = 1.0 / math.sqrt(height * rows * width)
    filter_grad, sign = last_filter(groups, parts, channels, scale, 0)
    input_grad = last_data(own, pieces, height, 0, (sign,))
    return (
        output,
        input_grad,
        filter_grad.reshape(3, 3, share, channels),
    )


def per_device(activations, weights, cotangent):
    local, height, width = activations.shape
    rows = lax.axis_size("rows")
    whole_tiles = local % 128 == 0 and width % 128 == 0 and (local // rows) % 16 == 0
    if whole_tiles and height == 2 and rows == 4:
        return fast(activations, weights, cotangent)
    return plain(activations, weights, cotangent)


def solution(mesh):
    placed = (P("chan", "rows", None), P(None, None, "chan", None), P("chan", "rows", None))
    return jax.shard_map(
        per_device,
        mesh=mesh,
        in_specs=placed,
        out_specs=(
            P("chan", "rows", None),
            P("chan", "rows", None),
            P(None, None, ("chan", "rows"), None),
        ),
        check_vma=False,
    )
```

```python
import functools
import math

import jax
import jax.numpy as jnp
from jax import lax
from jax.experimental import pallas as pl
from jax.experimental.pallas import tpu as pltpu
from jax.sharding import PartitionSpec as P

BF16, F32 = jnp.bfloat16, jnp.float32
SPAN = 124.0
LEAST = 2.0**-100
EXTRA = 16
VMEM_BYTES = 40 * 2**20


def call(body, outs, args, scratch=(), flops=0, after=(), far_out=()):
    def step(*refs):
        body(*refs[: len(args)], *refs[len(args) + len(after) :])

    return pl.pallas_call(
        step,
        out_shape=tuple(outs),
        in_specs=[pl.BlockSpec(memory_space=pltpu.VMEM)] * len(args)
        + [pl.BlockSpec(memory_space=pl.ANY)] * len(after),
        out_specs=tuple(pl.BlockSpec(memory_space=pltpu.HBM if i in far_out else pltpu.VMEM) for i in range(len(outs))),
        scratch_shapes=list(scratch),
        compiler_params=pltpu.CompilerParams(vmem_limit_bytes=VMEM_BYTES),
        cost_estimate=pl.CostEstimate(flops=int(flops), bytes_accessed=0, transcendentals=0),
    )(*args, *after)


def shape(dims, dtype):
    return jax.ShapeDtypeStruct(dims, dtype)


def rounded_up(top):
    return jnp.maximum(top * 1.01, LEAST).astype(BF16)


def put_coded(ref, columns, values):
    number = values.shape[0]
    size = jnp.abs(values)
    top = rounded_up(jnp.max(size, axis=0, keepdims=True))
    code = jnp.exp2(size * ((2 * SPAN) / top.astype(F32)) - SPAN)
    ref[:number, columns] = jnp.where(values < 0, -code, code).astype(BF16)
    ref[number:, columns] = jnp.broadcast_to(top, (EXTRA, values.shape[1]))


def get_coded(ref, columns, rows=None):
    number = ref.shape[0] - EXTRA
    rows = slice(0, number) if rows is None else rows
    step = ref[number:, columns].astype(F32)[:1] * (0.5 / SPAN)
    code = ref[rows, columns].astype(F32)
    size = (jnp.log2(jnp.abs(code)) + SPAN) * step
    return jnp.where(code < 0, -size, size)


def window_of(core, own, adj, halo, width):
    before = jnp.where(core == 0, halo, adj[:, -width:])
    after = jnp.where(core == 0, adj[:, :width], halo)
    return jnp.concatenate([before, own, after], axis=1)


def data_kernel(width, own_ref, adj_ref, halo_ref, w_ref, keep_ref, give_ref, left):
    core = lax.axis_index("rows") % 2
    y = lax.axis_index("chan") % 2
    local, cells = own_ref.shape
    slab = window_of(core, own_ref[...], adj_ref[...], halo_ref[...], width).astype(F32)
    turned = slab.T
    count = turned.shape[0]
    column = lax.broadcasted_iota(jnp.int32, turned.shape, 0) % width
    moved = [
        jnp.where(column == width - 1, 0.0, pltpu.roll(turned, count - 1, 0)),
        turned,
        jnp.where(column == 0, 0.0, pltpu.roll(turned, 1, 0)),
    ]
    moved = [m.astype(BF16) for m in moved]
    for a in range(3):
        for b in range(3):
            tap = 3 * a + b
            left[:, tap * local : (tap + 1) * local] = moved[b][(2 - a) * width : (2 - a) * width + cells]
    for z in range(w_ref.shape[1] // (2 * local)):
        sums = jnp.dot(left[...], w_ref[:, 2 * z * local : 2 * (z + 1) * local], preferred_element_type=F32)
        even, odd = sums[:, :local], sums[:, local:]
        here = slice(z * local, (z + 1) * local)
        keep_ref[:, here] = jnp.where(y == 0, even, odd)
        put_coded(give_ref, here, jnp.where(y == 0, odd, even))


def data_sums(own, adj, halo, taps, width, cost, after=()):
    local, cells = own.shape
    channels = taps.shape[1]
    outs = [shape((cells, channels // 2), F32), shape((cells + EXTRA, channels // 2), BF16)]
    return call(
        functools.partial(data_kernel, width), outs, (own, adj, halo, taps),
        [pltpu.VMEM((cells, 9 * local), BF16)], cost, after,
    )


def middle_kernel(come_ref, keep_ref, own_ref, *piece_refs):
    z = (lax.axis_index("chan") // 2)
    local = own_ref.shape[1]
    for k in range(len(piece_refs) + 1):
        here = pl.ds(pl.multiple_of((z ^ k) * local, local), local)
        total = keep_ref[:, here] + get_coded(come_ref, here)
        if k == 0:
            own_ref[...] = total
        else:
            put_coded(piece_refs[k - 1], slice(None), total)


def middle(come, keep, local, cost, after=()):
    cells, columns = keep.shape
    outs = [shape((cells, local), F32)] + [shape((cells + EXTRA, local), BF16)] * (columns // local - 1)
    return call(middle_kernel, outs, (come, keep), (), cost, after)


def put_rows(ref, values):
    width = ref.shape[2]
    for r in range(ref.shape[1]):
        ref[:, r, :] = values[:, r * width : (r + 1) * width].astype(BF16)


def last_data_kernel(own_ref, *refs):
    total = own_ref[...]
    for ref in refs[:-1]:
        total = total + get_coded(ref, slice(None))
    put_rows(refs[-1], total.T)


def last_data(own, pieces, height, cost, after=()):
    cells, local = own.shape
    outs = [shape((local, height, cells // height), BF16)]
    return call(last_data_kernel, outs, (own, *pieces), (), cost, after)[0]


def views(blocks):
    arrays, places = [], []
    for array, start in blocks:
        found = [i for i, held in enumerate(arrays) if held is array]
        if not found:
            arrays.append(array)
        places.append((found[0] if found else len(arrays) - 1, start))
    return arrays, places


def pair_of(y, near, far):
    return jnp.concatenate([jnp.where(y == 0, near, far), jnp.where(y == 0, far, near)], axis=0)


def lines_kernel(width, own_ref, adj_ref, halo_ref, rim_ref, left):
    row = lax.axis_index("rows")
    core, chip = row % 2, row // 2
    local, cells = own_ref.shape
    share = left.shape[0] // 18
    own, adj = own_ref[...], adj_ref[...]
    halo, rim = halo_ref[...], rim_ref[...]
    mine = window_of(core, own, adj, halo, width)
    theirs = window_of(1 - core, adj, own, rim, width)
    both = jnp.concatenate([mine, theirs], axis=1)
    place = lax.broadcasted_iota(jnp.int32, (2 * share, local), 0)
    wanted = jnp.where(place < share, chip * 2 + core, (1 - chip) * 2 + core) * share + place % share
    pick = (lax.broadcasted_iota(jnp.int32, (2 * share, local), 1) == wanted).astype(BF16)
    chosen = jnp.dot(pick, both, preferred_element_type=F32)
    count = chosen.shape[1]
    column = lax.broadcasted_iota(jnp.int32, chosen.shape, 1) % width
    moved = [
        jnp.where(column == width - 1, 0.0, pltpu.roll(chosen, count - 1, 1)),
        chosen,
        jnp.where(column == 0, 0.0, pltpu.roll(chosen, 1, 1)),
    ]
    moved = [m.astype(BF16) for m in moved]
    span = count // 2
    for part in range(2):
        for a in range(3):
            for b in range(3):
                tap = 3 * a + b
                start = part * span + (2 - a) * width
                for q in range(2):
                    left[q * 9 * share + tap * share : q * 9 * share + (tap + 1) * share,
                         part * cells : (part + 1) * cells] = moved[b][q * share : (q + 1) * share, start : start + cells]


def filter_lines(own, adj, halo, rim, share, width, cost, after=()):
    cells = own.shape[1]
    outs = [shape((18 * share, 2 * cells), BF16)]
    return call(functools.partial(lines_kernel, width), outs, (own, adj, halo, rim), (), cost, after)[0]


def stack_kernel(*refs):
    start = 0
    for ref in refs[:-1]:
        refs[-1][start : start + ref.shape[0]] = ref[...]
        start += ref.shape[0]


def stacked(blocks, cost, after=()):
    rows, columns = blocks[0].shape
    return call(stack_kernel, [shape((len(blocks) * rows, columns), BF16)], blocks, (), cost, after)[0]


def filter_kernel(places, left, *refs):
    y = lax.axis_index("chan") % 2
    keep_ref, give_ref = refs[-2:]
    share = keep_ref.shape[0] // 9
    pairs = len(places) // 4
    local = keep_ref.shape[1] // (2 * pairs)
    held = [refs[i][start : start + local] for i, start in places]
    near, far, near_o, far_o = (held[i * pairs : (i + 1) * pairs] for i in range(4))
    for t in range(pairs):
        right = jnp.concatenate(
            [pair_of(y, near[t], far[t]), pair_of(y, near_o[t], far_o[t])], axis=1
        )
        here = slice(t * 2 * local, (t + 1) * 2 * local)
        for q in (1, 0):
            sums = lax.dot_general(
                left[q * 9 * share : (q + 1) * 9 * share], right, (((1,), (1,)), ((), ())), preferred_element_type=F32
            )
            if q:
                put_coded(give_ref, here, sums)
            else:
                keep_ref[:, here] = sums


def filter_sums(lines, near, far, near_o, far_o, local, cost, after=()):
    share, pairs = lines.shape[0] // 18, len(near)
    arrays, places = views([*near, *far, *near_o, *far_o])
    outs = [shape((9 * share, pairs * 2 * local), F32), shape((9 * share + EXTRA, pairs * 2 * local), BF16)]
    return call(functools.partial(filter_kernel, places), outs, (lines, *arrays), (), cost, after)


def last_filter_kernel(groups, scale, *refs):
    z = lax.axis_index("chan") // 2
    out_far, sign_ref, done_ref, sent = refs[-4:]
    sign_ref[...] = jnp.zeros_like(sign_ref)
    step = done_ref.shape[1] // sum(groups)
    lines = done_ref.shape[0] // 3
    copies = []
    for a in range(3):
        rows = slice(a * lines, (a + 1) * lines)
        t = 0
        for i, pairs in enumerate(groups):
            for j in range(pairs):
                here = slice(j * step, (j + 1) * step)
                there = pl.ds(pl.multiple_of((z ^ t) * step, step), step)
                done_ref[rows, there] = (refs[2 * i][rows, here] + get_coded(refs[2 * i + 1], here, rows)) * scale
                t += 1
        copies.append(pltpu.make_async_copy(done_ref.at[rows], out_far.at[rows], sent.at[a]))
        copies[-1].start()
    for copy in copies:
        copy.wait()


def last_filter(groups, parts, channels, scale, cost, after=()):
    size = (parts[0].shape[0], channels)
    scratch = [pltpu.VMEM(size, F32), pltpu.SemaphoreType.DMA((3,))]
    kernel = functools.partial(last_filter_kernel, groups, scale)
    return call(kernel, [shape(size, F32), shape((8, 128), F32)], parts, scratch, cost, after, far_out=(0,))


def output_kernel(places, cells, width, w_ref, *refs):
    core = lax.axis_index("rows") % 2
    chan = lax.axis_index("chan")
    y, z = chan % 2, chan // 2
    inner_ref, edge_ref, xs, xo = refs[-4:]
    pairs = len(places) // 4
    local = w_ref.shape[2] // (2 * pairs)
    held = [refs[i][start : start + local] for i, start in places]
    near, far, near_o, far_o = (held[i * pairs : (i + 1) * pairs] for i in range(4))
    for t in range(pairs):
        there = pl.ds(pl.multiple_of((z ^ t) * 2 * local, 2 * local), 2 * local)
        xs[there, :] = pair_of(y, near[t], far[t])
        other = pair_of(y, near_o[t], far_o[t])
        xo[there, :] = jnp.where(core == 0, other[:, :width], other[:, -width:])
    filters = w_ref.shape[1]
    w = w_ref[...].reshape(9 * filters, w_ref.shape[2])
    parts = jnp.dot(w, xs[...], preferred_element_type=F32)
    beside = w_ref[pl.ds(jnp.where(core == 0, 6, 0), 3)].reshape(3 * filters, w_ref.shape[2])
    more = jnp.dot(beside, xo[...], preferred_element_type=F32)
    rows = cells // width
    lines = [[None] * 3 for _ in range(rows + 2)]
    for a in range(3):
        for r in range(rows):
            for b in range(3):
                tap = 3 * a + b
                value = parts[tap * filters : (tap + 1) * filters, r * width : (r + 1) * width]
                line = lines[r - a + 2]
                line[b] = value if line[b] is None else line[b] + value
    for b in range(3):
        value = more[b * filters : (b + 1) * filters]
        lines[rows][b] = lines[rows][b] + jnp.where(core == 0, value, 0.0)
        lines[1][b] = lines[1][b] + jnp.where(core == 0, 0.0, value)
    column = lax.broadcasted_iota(jnp.int32, (filters, width), 1)
    total = []
    for line in lines:
        left = jnp.where(column == 0, 0.0, pltpu.roll(line[0], 1, 1))
        right = jnp.where(column == width - 1, 0.0, pltpu.roll(line[2], width - 1, 1))
        total.append(left + line[1] + right)
    for r in range(rows):
        inner_ref[:, r * width : (r + 1) * width] = total[r + 1]
    edge_ref[...] = jnp.where(core == 0, total[0], total[-1])


def output_sums(taps, near, far, near_o, far_o, width, cost, after=()):
    filters, channels = taps.shape[1:]
    arrays, places = views([*near, *far, *near_o, *far_o])
    cells = arrays[0].shape[1]
    outs = [shape((filters, cells), F32), shape((filters, width), F32)]
    return call(
        functools.partial(output_kernel, places, cells, width), outs, (taps, *arrays),
        [pltpu.VMEM((channels, cells), BF16), pltpu.VMEM((channels, width), BF16)],
        cost, after,
    )


def last_output_kernel(inner_ref, edge_ref, out_ref):
    core = lax.axis_index("rows") % 2
    edge = edge_ref[...]
    zero = jnp.zeros_like(edge)
    top, bottom = jnp.where(core == 0, edge, zero), jnp.where(core == 0, zero, edge)
    middle_rows = [zero] * (out_ref.shape[1] - 2)
    put_rows(out_ref, inner_ref[...] + jnp.concatenate([top, *middle_rows, bottom], axis=1))


def last_output(inner, edge, cost, after=()):
    filters, width = edge.shape
    outs = [shape((filters, inner.shape[1] // width, width), BF16)]
    return call(last_output_kernel, outs, (inner, edge), (), cost, after)[0]


def exchange(x, axis, distance):
    size = lax.axis_size(axis)
    return lax.ppermute(x, axis, [(i, i ^ distance) for i in range(size)])


def shift_columns(values, offset):
    if offset == 0:
        return values
    extent = values.shape[-1]
    widths = [(0, 0)] * (values.ndim - 1)
    if offset > 0:
        return jnp.pad(values[..., offset:], widths + [(0, offset)])
    return jnp.pad(values[..., : extent + offset], widths + [(-offset, 0)])


def encode(values):
    top = jnp.maximum(jnp.max(jnp.abs(values), axis=0, keepdims=True) * 1.01, LEAST)
    top = lax.reduce_precision(top, 8, 7)
    factor = (2 * SPAN) / top
    code = jnp.exp2(jnp.abs(values) * factor - SPAN)
    code = jnp.where(values < 0, -code, code).astype(BF16)
    return jnp.concatenate([code, jnp.broadcast_to(top.astype(BF16), (16, top.shape[1]))], axis=0)


def decode(coded):
    number = coded.shape[0] - 16
    step = coded[number : number + 1].astype(F32) * (0.5 / SPAN)
    code = coded[:number].astype(F32)
    size = (jnp.log2(jnp.abs(code)) + SPAN) * step
    return jnp.where(code < 0, -size, size)


def gathered(x):
    size, me = lax.axis_size("chan"), lax.axis_index("chan")
    blocks = jnp.stack([x] + [exchange(x, "chan", k) for k in range(1, size)])
    bit = 1
    while bit < size:
        pairs = blocks.reshape((-1, 2, bit) + x.shape)
        swapped = jnp.stack([pairs[:, 1], pairs[:, 0]], axis=1)
        blocks = jnp.where((me // bit) % 2 == 1, swapped, pairs).reshape(blocks.shape)
        bit *= 2
    return blocks.reshape((size * x.shape[0],) + x.shape[1:])


def plain(activations, weights, cotangent):
    local, height, width = activations.shape
    chans, rows = lax.axis_size("chan"), lax.axis_size("rows")
    chips, zs = rows // 2, chans // 2
    me, row = lax.axis_index("chan"), lax.axis_index("rows")
    core, chip = row % 2, row // 2
    own_y, own_z = me % 2, me // 2
    first = core == 0
    share = local // rows
    channels = weights.shape[3]
    cells = height * rows * width
    taps = weights.reshape(9, local, channels)

    edges = [(i, i + 1) for i in range(1, rows - 1, 2)]
    edge = jnp.where(first, cotangent[:, 0], cotangent[:, height - 1])
    halo = lax.ppermute(edge, "rows", edges + [(j, i) for i, j in edges])
    mine = jnp.concatenate([cotangent, halo[:, None]], axis=1)
    other = exchange(mine, "rows", 1)
    low, high = jnp.where(first, mine, other), jnp.where(first, other, mine)
    slab = jnp.concatenate([low[:, height:], low[:, :height], high], axis=1)

    xs = gathered(activations.reshape(local, height * width))
    xo = exchange(xs, "rows", 1)
    xchip = jnp.concatenate([jnp.where(first, xs, xo), jnp.where(first, xo, xs)], axis=1)

    window = jnp.where(first, slab[:, : height + 2], slab[:, height:])
    shifted = [shift_columns(window, 1 - b) for b in range(3)]
    stack = jnp.concatenate(
        [shifted[b][:, 2 - a : 2 - a + height].reshape(local, -1) for a in range(3) for b in range(3)], axis=0
    )
    partial = lax.dot_general(
        stack, taps.reshape(9 * local, channels), (((0,), (0,)), ((), ())), preferred_element_type=F32
    )
    pairs = partial.reshape(height * width, zs, 2, local)
    keep = jnp.where(own_y == 0, pairs[:, :, 0], pairs[:, :, 1]).reshape(height * width, zs * local)
    give = jnp.where(own_y == 0, pairs[:, :, 1], pairs[:, :, 0]).reshape(height * width, zs * local)
    total = keep + decode(exchange(encode(give), "chan", 1))
    coded = encode(total)
    grad = lax.dynamic_slice_in_dim(total, own_z * local, local, axis=1)
    for k in range(1, zs):
        piece = lax.dynamic_slice_in_dim(coded, (own_z ^ k) * local, local, axis=1)
        grad = grad + decode(exchange(piece, "chan", 2 * k))
    input_grad = grad.T.reshape(local, height, width).astype(BF16)

    def half(x, axis):
        shape = x.shape[:axis] + (chips, 2, share) + x.shape[axis + 1 :]
        x = x.reshape(shape)
        return jnp.where(first, lax.index_in_dim(x, 0, axis + 1, False), lax.index_in_dim(x, 1, axis + 1, False))

    gs = half(slab, 0)
    moved = [shift_columns(gs, 1 - b) for b in range(3)]
    lines = jnp.stack(
        [moved[b][:, :, 2 - a : 2 - a + 2 * height].reshape(chips, share, -1) for a in range(3) for b in range(3)],
        axis=1,
    )
    sums = lax.dot_general(
        lines.reshape(chips * 9 * share, -1), xchip, (((1,), (1,)), ((), ())), preferred_element_type=F32
    ).reshape(chips, 9 * share, channels)
    filter_sum = lax.dynamic_index_in_dim(sums, chip, 0, False)
    for k in range(1, chips):
        piece = encode(lax.dynamic_index_in_dim(sums, chip ^ k, 0, False))
        filter_sum = filter_sum + decode(exchange(piece, "rows", 2 * k))
    filter_grad = (filter_sum * (1.0 / math.sqrt(cells))).reshape(3, 3, share, channels)

    wh = half(taps, 1).reshape(9 * chips * share, channels)
    parts = lax.dot_general(wh, xchip, (((1,), (0,)), ((), ())), preferred_element_type=F32)
    parts = parts.reshape(3, 3, chips * share, 2 * height, width)
    line = sum(shift_columns(
        sum(jnp.pad(parts[a, b], ((0, 0), (2 - a, a), (0, 0))) for a in range(3)), b - 1) for b in range(3))
    up = [(i, i + 2) for i in range(rows - 2)]
    above = lax.ppermute(line[:, -1], "rows", up)
    below = lax.ppermute(line[:, 0], "rows", [(j, i) for i, j in up])
    inner = line[:, 1:-1]
    inner = inner.at[:, 0].add(above).at[:, -1].add(below).astype(BF16)
    stay = jnp.where(first, inner[:, :height], inner[:, height:])
    go = jnp.where(first, inner[:, height:], inner[:, :height])
    come = exchange(go, "rows", 1)
    stay, come = (x.reshape(chips, share, height, width) for x in (stay, come))
    output = jnp.stack([jnp.where(first, stay, come), jnp.where(first, come, stay)], axis=1)
    return output.reshape(local, height, width), input_grad, filter_grad


def fast(activations, weights, cotangent):
    local, height, width = activations.shape
    chans, rows = lax.axis_size("chan"), lax.axis_size("rows")
    zs, share, channels = chans // 2, local // rows, weights.shape[3]
    first = lax.axis_index("rows") % 2 == 0
    taps = weights.reshape(9, local, channels)

    edges = [(i, i + 1) for i in range(1, rows - 1, 2)]
    edges += [(j, i) for i, j in edges]
    g = cotangent.reshape(local, height * width)
    edge = jnp.where(first, g[:, :width], g[:, -width:])
    halo = lax.ppermute(edge, "rows", edges)
    adj = exchange(g, "rows", 1)
    x = activations.reshape(local, height * width)

    half = zs // 2
    direct = {0: x}
    for k in (1, 3, 2, 6, 4):
        direct[k] = exchange(x, "chan", k)

    keep, give = data_sums(g, adj, halo, taps.reshape(9 * local, channels), width, 24000000000.0)
    come = exchange(give, "chan", 1)

    others = {k: exchange(direct[k], "rows", 1) for k in range(2 * half)}
    rim = exchange(halo, "rows", 1)
    g_after, give = lax.optimization_barrier((g, give))
    lines = filter_lines(g_after, adj, halo, rim, share, width, 12000000000.0)
    near = [(direct[2 * t], 0) for t in range(half)]
    far = [(direct[2 * t + 1], 0) for t in range(half)]
    near_o = [(others[2 * t], 0) for t in range(half)]
    far_o = [(others[2 * t + 1], 0) for t in range(half)]
    mine, gift = filter_sums(lines, near, far, near_o, far_o, local, 0)
    far_z = jnp.concatenate([direct[2 * t] for t in range(half, zs)], axis=0)
    far_z, give = lax.optimization_barrier((far_z, give))
    far_zy = exchange(far_z, "chan", 1)
    far_zo, far_zyo = exchange(far_z, "rows", 1), exchange(far_zy, "rows", 1)
    near2 = [(far_z, t * local) for t in range(zs - half)]
    far2 = [(far_zy, t * local) for t in range(zs - half)]
    near2_o = [(far_zo, t * local) for t in range(zs - half)]
    far2_o = [(far_zyo, t * local) for t in range(zs - half)]
    own, *pieces = middle(come, keep, local, 0)
    pieces = [exchange(piece, "chan", 2 * k) for k, piece in enumerate(pieces, 1)]
    mine2, gift2 = filter_sums(lines, near2, far2, near2_o, far2_o, local, 0)
    parts = [mine, exchange(gift, "rows", 2), mine2, exchange(gift2, "rows", 2)]
    groups = (half, zs - half)
    inner, rest = output_sums(taps, near + near2, far + far2, near_o + near2_o, far_o + far2_o, width, 0)
    output = last_output(inner, lax.ppermute(rest, "rows", edges), 0)

    scale = 1.0 / math.sqrt(height * rows * width)
    filter_grad, sign = last_filter(groups, parts, channels, scale, 0)
    input_grad = last_data(own, pieces, height, 0, (sign,))
    return (
        output,
        input_grad,
        filter_grad.reshape(3, 3, share, channels),
    )


def per_device(activations, weights, cotangent):
    local, height, width = activations.shape
    rows = lax.axis_size("rows")
    whole_tiles = local % 128 == 0 and width % 128 == 0 and (local // rows) % 16 == 0
    if whole_tiles and height == 2 and rows == 4:
        return fast(activations, weights, cotangent)
    return plain(activations, weights, cotangent)


def solution(mesh):
    placed = (P("chan", "rows", None), P(None, None, "chan", None), P("chan", "rows", None))
    return jax.shard_map(
        per_device,
        mesh=mesh,
        in_specs=placed,
        out_specs=(
            P("chan", "rows", None),
            P("chan", "rows", None),
            P(None, None, ("chan", "rows"), None),
        ),
        check_vma=False,
    )
```
